32 devices in a mesh: energy: 4 (over z), slab: 8 (over y, x, core).
Axes of the slice: x: 2, y: 2, z: 4, core: 2. Of those that a mesh axis runs over, the one named last changes fastest.
Arguments:
- hamiltonian: float32 [2048, 256], P('slab'), as said below
- decay: float32 [8, 256], P('slab'), may hold values from 0 to 1, as said below
- coupling: float32 [8, 256], P('slab'), may hold values from 0.2 to 2
- rows: int32 [8, 32], P('slab'), may hold values from 0 to 255
- screened: float32 [8, 32, 32, 256], P('slab', None, 'energy'), may hold values from -1 to 1
Outputs:
- sigma: float32 [32, 256, 256], P('energy', 'slab')
The draws below stay inside these ranges and needn't reach their ends.
Inputs may be any that keep to these rules, and one draw needn't show every extreme that they name: `hamiltonian`: entries are independent and small enough that every H_s / z_k has spectral radius well under one. `decay`: every entry lies strictly between 0 and 1.
All inputs are finite; a program needn't handle non-finite values.
Results may differ from the reference program's by a relative error of at most 0.0001.
Values sent between devices are 32-bit elements; how exact they have to be, the bound alone decides.
A program may use at most 128 MiB of HBM per device.

```python
import math
import jax
import jax.numpy as jnp
from jax import lax

BS = 256
NR = 32
NS_ITERS = 2
LAYER_NUMBER = 8
NE = 32


def draw_hamiltonian(key, part):
    extent = (LAYER_NUMBER * BS, BS)
    deviation = 1.0 / (3.0 * math.sqrt(BS))
    values = jnp.clip(jax.random.normal(key, extent, jnp.float32), -3.0, 3.0) * deviation
    return values


def draw_decay(key, part):
    keys = jax.random.split(key, 6)
    fraction_share = 0.5
    lasting = jax.random.uniform(keys[0], (BS,), jnp.float32) < fraction_share
    slow_rate = jax.random.uniform(keys[1], (BS,), jnp.float32, 0.1, 0.5) / LAYER_NUMBER
    fast_rate = jax.random.uniform(keys[2], (BS,), jnp.float32, 1.0, 3.0)
    rates_base = jnp.where(lasting, slow_rate, fast_rate)
    variation = jax.random.uniform(keys[3], (LAYER_NUMBER, BS), jnp.float32, 0.6, 1.6)
    density_averages = jax.random.randint(keys[4], (2,), 0, LAYER_NUMBER)
    packet_batches = jnp.any(jnp.arange(LAYER_NUMBER)[:, None] == density_averages[None, :], axis=1)
    broadening_parts = jax.random.uniform(keys[5], (LAYER_NUMBER, BS), jnp.float32, 0.5, 0.8)
    scaling_factors = jnp.where(packet_batches[:, None], broadening_parts, 1.0)
    return jnp.exp(-rates_base[None, :] * variation) * scaling_factors


def place_ends(drawn, own_key, smallest, largest):
    place = [jax.random.randint(jax.random.fold_in(own_key, axis), (), 0, length) for axis, length in enumerate(drawn.shape)]
    longest = drawn.shape.index(max(drawn.shape))
    neighbour = place[:longest] + [(place[longest] + 1) % drawn.shape[longest]] + place[longest + 1:]
    return drawn.at[tuple(place)].set(smallest).at[tuple(neighbour)].set(largest)


def level_of(key, shape, shards, least, top_value):
    loudness = 1.0
    for dim, blocks in shards:
        steps = jax.random.uniform(jax.random.fold_in(jax.random.fold_in(key, 6), dim), (blocks,), jnp.float32, least / len(shards), top_value / len(shards))
        loudness = loudness * jnp.repeat(jnp.exp(steps), shape[dim] // blocks).reshape((-1,) + (1,) * (len(shape) - 1 - dim))
    return loudness


def scatter_about(key, shape, scale, reach, shards=(), held_as=jnp.bfloat16):
    result = jax.random.normal(key, shape, jnp.float32) * scale
    if len(shards) > 0:
        result = level_of(key, shape, shards, -0.22, 0.18) * result
    return jnp.clip(result, min=-reach, max=reach).astype(held_as)


def setup_inputs(seed: int = 0) -> dict:
    arg_keys = jax.random.split(jax.random.key(seed), 6)
    hamiltonian = draw_hamiltonian(jax.random.fold_in(arg_keys[5], 71), 0)
    decay = draw_decay(jax.random.fold_in(arg_keys[5], 71), 0)
    coupling = jnp.clip(jnp.exp(math.log(2.0) - 2.3025851 * jax.random.uniform(arg_keys[2], (LAYER_NUMBER, BS), jnp.float32) ** level_of(arg_keys[2], (LAYER_NUMBER, BS), ((0, 8),), -0.2, 0.2)), 0.2, 2.0)
    rows = place_ends(jax.random.randint(arg_keys[3], (LAYER_NUMBER, NR), 0, BS), jax.random.fold_in(arg_keys[3], 1), 0, BS - 1).astype(jnp.int32)
    screened = scatter_about(arg_keys[4], (LAYER_NUMBER, NE, NR, BS), NE ** -0.5, 1.0, ((0, 8), (2, 4)), jnp.float32)
    return dict(hamiltonian=hamiltonian, decay=decay, coupling=coupling, rows=rows, screened=screened)


FULL_PRECISION = lax.Precision.HIGHEST


def local_green(hamilton_block, shifts):
    identity = jnp.eye(hamilton_block.shape[0], dtype=jnp.float32)
    column = shifts[:, None, None]
    green_block = (identity[None] + hamilton_block[None] / column) / column
    for sweep_index in range(NS_ITERS):
        applied = jnp.einsum("ij,kjl->kil", hamilton_block, green_block, precision=FULL_PRECISION)
        shifted = column * green_block - applied
        green_block = 2.0 * green_block - jnp.einsum("kij,kjl->kil", green_block, shifted, precision=FULL_PRECISION)
    return green_block


def reference(hamiltonian, decay, coupling, rows, screened):
    shifts = 1.0 + jnp.arange(NE, dtype=jnp.float32) / NE
    hamilton_blocks = hamiltonian.reshape(LAYER_NUMBER, BS, BS)

    def diagonals(hamilton_block):
        return jnp.diagonal(local_green(hamilton_block, shifts), axis1=1, axis2=2)

    diag_all = lax.map(diagonals, hamilton_blocks)
    injection_contributions = coupling[:, None, :] * diag_all / LAYER_NUMBER

    def advance(carried, inputs):
        decay_row, source_row = inputs
        return decay_row[None, :] * carried + source_row, carried

    _, incoming = lax.scan(advance, jnp.zeros((NE, BS), jnp.float32), (decay, injection_contributions))

    def slab_sigma(inputs):
        hamilton_block, entering, chosen, interaction = inputs
        green_block = local_green(hamilton_block, shifts)
        picked = jnp.take(green_block, chosen, axis=1)
        dressed = picked + jnp.einsum("kri,kij->krj", picked * entering[:, None, :], green_block, precision=FULL_PRECISION)
        product = jnp.fft.fft(dressed, axis=0) * jnp.fft.fft(interaction, axis=0)
        return jnp.real(jnp.fft.ifft(product, axis=0)).astype(jnp.float32)

    sigma_all = lax.map(slab_sigma, (hamilton_blocks, incoming, rows, screened))
    return jnp.transpose(sigma_all, (1, 0, 2, 3)).reshape(NE, LAYER_NUMBER * NR, BS)
```

```python
import functools

import jax
import jax.numpy as jnp
from jax import lax
from jax.experimental import pallas as pl
from jax.experimental.pallas import tpu as pltpu
from jax.sharding import PartitionSpec as P

MESH = pl.DeviceIdType.MESH
POWERS = 8
SUBLANES = 8


def split(a):
    high = a.astype(jnp.bfloat16)
    return high, (a - high.astype(jnp.float32)).astype(jnp.bfloat16)


def mul(a, b):
    (a_high, a_low), (b_high, b_low) = a, b
    dot = functools.partial(jnp.dot, preferred_element_type=jnp.float32)
    return dot(a_high, b_high) + (dot(a_high, b_low) + dot(a_low, b_high))


def partner_of(place, step, count):
    if count & (count - 1):
        return lax.rem(place + step, count)
    bit = 1
    while bit <= step:
        if step & bit:
            place = place + bit - 2 * bit * lax.rem(lax.div(place, bit), 2)
        bit *= 2
    return place


def kernel(
    energies, slabs, rows_ref, decay_ref, coupling_ref, hamilton_ref, screened_ref, out_ref,
    hamilton, square, screen, dressed, sigma, decays, terms,
    in_sem, decay_send, decay_recv, term_send, term_recv, sigma_send, sigma_recv, own_sem,
):
    energy, slab = lax.axis_index("energy"), lax.axis_index("slab")
    total, lines, width = screen.shape
    share = total // energies

    barrier = pltpu.get_barrier_semaphore()
    for step in range(1, slabs):
        pl.semaphore_signal(
            barrier, inc=1, device_id=(energy, partner_of(slab, step, slabs)), device_id_type=MESH
        )
    for step in range(1, energies):
        pl.semaphore_signal(
            barrier, inc=1, device_id=(partner_of(energy, step, energies), slab), device_id_type=MESH
        )
    load_hamilton = pltpu.make_async_copy(hamilton_ref, hamilton, in_sem.at[0])
    load_screen = pltpu.make_async_copy(screened_ref, screen, in_sem.at[1])
    load_hamilton.start()
    load_screen.start()
    decays[slab] = jnp.broadcast_to(decay_ref[...], (POWERS, width))

    load_hamilton.wait()
    h1 = hamilton[...]
    t1 = h1.T
    h1s, t1s = split(h1), split(t1)
    h2 = mul(h1s, h1s)
    t2 = mul(t1s, t1s)
    h2s, t2s = split(h2), split(t2)
    h4 = mul(h2s, h2s)
    t3 = mul(t2s, t1s)
    square[...] = h2

    def trace(product):
        return jnp.sum(product, axis=0, keepdims=True)

    eye = lax.broadcasted_iota(jnp.int32, h1.shape, 0) == lax.broadcasted_iota(jnp.int32, h1.shape, 1)
    diagonals = jnp.concatenate(
        [
            jnp.ones((1, width), jnp.float32),
            trace(jnp.where(eye, h1, 0.0)),
            trace(t1 * h1),
            trace(t1 * h2),
            trace(t2 * h2),
            trace(t1 * h4),
            trace(t2 * h4),
            trace(t3 * h4),
        ],
        axis=0,
    )
    terms[slab] = diagonals * (coupling_ref[...] / slabs)

    pl.semaphore_wait(barrier, slabs + energies - 2)
    gathers = []
    for step in range(1, slabs):
        target = (energy, partner_of(slab, step, slabs))
        for held, send, recv in ((terms, term_send, term_recv), (decays, decay_send, decay_recv)):
            copy = pltpu.make_async_remote_copy(
                src_ref=held.at[slab], dst_ref=held.at[slab], send_sem=send.at[step], recv_sem=recv.at[step],
                device_id=target, device_id_type=MESH,
            )
            copy.start()
            gathers.append(copy)

    h4s = split(h4)
    lane = lax.broadcasted_iota(jnp.int32, (1, width), 1)
    chosen = [rows_ref[0, energy * lines + line] for line in range(lines)]
    v0 = jnp.concatenate([(lane == row).astype(jnp.float32) for row in chosen], axis=0)
    v1 = jnp.concatenate([hamilton[pl.ds(row, 1), :] for row in chosen], axis=0)
    v2 = jnp.concatenate([square[pl.ds(row, 1), :] for row in chosen], axis=0)
    v3 = mul(split(v1), h2s)
    lower = jnp.concatenate([v0, v1, v2, v3], axis=0)
    upper = mul(split(lower), h4s)
    v = [lower[p * lines:(p + 1) * lines] for p in range(4)] + [upper[p * lines:(p + 1) * lines] for p in range(4)]
    inverses = [1.0 / (1.0 + k / total) for k in range(total)]
    picked = []
    for inverse in inverses:
        value = v[POWERS - 1]
        for p in reversed(range(POWERS - 1)):
            value = value * inverse + v[p]
        picked.append(value * inverse)

    for copy in gathers:
        copy.wait()
    carried = jnp.zeros((POWERS, width), jnp.float32)
    for place in range(slabs - 1):
        carried = jnp.where(place < slab, decays[place] * carried + terms[place], carried)
    entering = []
    inverse_rows = 1.0 / (1.0 + lax.broadcasted_iota(jnp.int32, (total, width), 0).astype(jnp.float32) / total)
    incoming = jnp.broadcast_to(carried[POWERS - 1:], (total, width))
    for p in reversed(range(POWERS - 1)):
        incoming = incoming * inverse_rows + carried[p:p + 1]
    incoming = incoming * inverse_rows
    for k in range(total):
        entering.append(picked[k] * incoming[k:k + 1])
    u = jnp.concatenate(entering, axis=0)
    scale = 1.0 / (
        1.0 + (lax.broadcasted_iota(jnp.int32, u.shape, 0) // lines).astype(jnp.float32) / total
    )
    u = u + scale * mul(split(u), h1s)
    scale2 = scale * scale
    u = u + scale2 * mul(split(u), h2s)
    u = u + (scale2 * scale2) * mul(split(u), h4s)
    u = (jnp.concatenate(picked, axis=0) + scale * u).reshape(total, lines, width)
    dressed[pl.ds(0, total)] = u
    dressed[pl.ds(total, total)] = u

    load_screen.wait()

    def convolve(place):
        first = place * share

        def add(m, acc):
            return acc + dressed[pl.ds(total + first - m, share)] * screen[m][None]

        return lax.fori_loop(0, total, add, jnp.zeros((share, lines, width), jnp.float32), unroll=4)

    mine = pl.ds(pl.multiple_of(energy * lines, SUBLANES), lines)
    order = sorted(range(1, energies), key=lambda step: (step < energies // 2, step))
    sends = []
    for step in order:
        place = partner_of(energy, step, energies)
        sigma[step] = convolve(place)
        copy = pltpu.make_async_remote_copy(
            src_ref=sigma.at[step], dst_ref=out_ref.at[:, mine, :],
            send_sem=sigma_send.at[step], recv_sem=sigma_recv.at[step],
            device_id=(place, slab), device_id_type=MESH,
        )
        copy.start()
        sends.append(copy)
    sigma[0] = convolve(energy)
    own = pltpu.make_async_copy(sigma.at[0], out_ref.at[:, mine, :], own_sem)
    own.start()
    for copy in sends:
        copy.wait()
    own.wait()


def fused(energies, slabs, hamiltonian, decay, coupling, rows, screened):
    total, lines, width = screened.shape
    share = total // energies
    any_space, vmem = pl.BlockSpec(memory_space=pl.ANY), pl.BlockSpec(memory_space=pltpu.VMEM)
    dma = pltpu.SemaphoreType.DMA
    return pl.pallas_call(
        functools.partial(kernel, energies, slabs),
        out_shape=jax.ShapeDtypeStruct((share, lines * energies, width), jnp.float32),
        in_specs=[pl.BlockSpec(memory_space=pltpu.SMEM), vmem, vmem, any_space, any_space],
        out_specs=any_space,
        scratch_shapes=[
            pltpu.VMEM((width, width), jnp.float32),
            pltpu.VMEM((width, width), jnp.float32),
            pltpu.VMEM((total, lines, width), jnp.float32),
            pltpu.VMEM((2 * total, lines, width), jnp.float32),
            pltpu.VMEM((energies, share, lines, width), jnp.float32),
            pltpu.VMEM((slabs, POWERS, width), jnp.float32),
            pltpu.VMEM((slabs, POWERS, width), jnp.float32),
            dma((2,)),
            dma((slabs,)),
            dma((slabs,)),
            dma((slabs,)),
            dma((slabs,)),
            dma((energies,)),
            dma((energies,)),
            dma,
        ],
        compiler_params=pltpu.CompilerParams(
            collective_id=0, has_side_effects=True, vmem_limit_bytes=32 * 1024 * 1024
        ),
    )(rows, decay, coupling, hamiltonian, screened)


def unfused(energies, slabs, hamiltonian, decay, coupling, rows, screened):
    total, lines, width = screened.shape
    share = total // energies
    dot = functools.partial(jnp.dot, precision=lax.Precision.HIGHEST)
    powers = [jnp.eye(width, dtype=jnp.float32)]
    for _ in range(POWERS - 1):
        powers.append(dot(powers[-1], hamiltonian))
    powers = jnp.stack(powers)
    own = coupling * jnp.diagonal(powers, axis1=1, axis2=2) / slabs
    decays = lax.all_gather(decay, "slab", axis=0, tiled=True)
    terms = lax.all_gather(own[None], "slab", axis=0, tiled=True)
    slab = lax.axis_index("slab")

    def advance(place, carried):
        return jnp.where(place < slab, decays[place] * carried + terms[place], carried)

    carried = lax.fori_loop(0, slabs - 1, advance, jnp.zeros_like(own))
    shifts = 1.0 + jnp.arange(total, dtype=jnp.int32).astype(jnp.float32) / total
    weights = shifts[:, None] ** -(1.0 + jnp.arange(POWERS, dtype=jnp.float32))
    incoming = dot(weights, carried)
    chosen = lax.dynamic_slice_in_dim(rows[0], lax.axis_index("energy") * lines, lines)
    picked = jnp.einsum("kp,prj->krj", weights, jnp.take(powers, chosen, axis=1), precision=lax.Precision.HIGHEST)
    scale = 1.0 / shifts[:, None, None]
    u = picked * incoming[:, None, :]
    u = u + scale * dot(u, powers[1])
    u = u + scale**2 * dot(u, powers[2])
    u = u + scale**4 * dot(u, powers[4])
    dressed = picked + scale * u

    def convolve(m, acc):
        return acc + jnp.roll(dressed, m, axis=0) * screened[m][None]

    sigma = lax.fori_loop(0, total, convolve, jnp.zeros_like(dressed))
    return lax.all_to_all(sigma, "energy", split_axis=0, concat_axis=1, tiled=True)


def solution(mesh):
    energies, slabs = mesh.shape["energy"], mesh.shape["slab"]

    def shards(hamiltonian, decay, coupling, rows, screened):
        lines = screened.shape[2]
        form = unfused if lines % SUBLANES else fused
        return form(energies, slabs, hamiltonian, decay, coupling, rows, screened[0])

    in_specs = (
        P("slab", None),
        P("slab", None),
        P("slab", None),
        P("slab", None),
        P("slab", None, "energy", None),
    )
    out_specs = P("energy", "slab", None)
    return jax.shard_map(shards, mesh=mesh, in_specs=in_specs, out_specs=out_specs, check_vma=False)
```

```python
import functools

import jax
import jax.numpy as jnp
from jax import lax
from jax.experimental import pallas as pl
from jax.experimental.pallas import tpu as pltpu
from jax.sharding import PartitionSpec as P

MESH = pl.DeviceIdType.MESH
POWERS = 8
SUBLANES = 8


def split(a):
    high = a.astype(jnp.bfloat16)
    return high, (a - high.astype(jnp.float32)).astype(jnp.bfloat16)


def mul(a, b):
    (a_high, a_low), (b_high, b_low) = a, b
    dot = functools.partial(jnp.dot, preferred_element_type=jnp.float32)
    return dot(a_high, b_high) + (dot(a_high, b_low) + dot(a_low, b_high))


def partner_of(place, step, count):
    bit = 1
    while bit <= step:
        if step & bit:
            place = place + bit - 2 * bit * lax.rem(lax.div(place, bit), 2)
        bit *= 2
    return place


def kernel(
    energies, slabs, rows_hbm, decay_hbm, coupling_hbm, hamilton_ref, screened_ref, out_ref,
    rows_ref, decay_ref, coupling_ref, hamilton, square, screen, dressed, sigma, decays, terms,
    in_sem, decay_send, decay_recv, term_send, term_recv, sigma_send, sigma_recv, own_sem,
):
    energy, slab = lax.axis_index("energy"), lax.axis_index("slab")
    total, lines, width = screen.shape
    share = total // energies

    loads = [
        pltpu.make_async_copy(source, held, in_sem.at[place])
        for place, (source, held) in enumerate(
            [
                (hamilton_ref, hamilton),
                (coupling_hbm, coupling_ref),
                (decay_hbm, decay_ref),
                (rows_hbm, rows_ref),
                (screened_ref, screen),
            ]
        )
    ]
    for load in loads:
        load.start()
    load_hamilton, load_coupling, load_decay, load_rows, load_screen = loads

    barrier = pltpu.get_barrier_semaphore()
    partners = [partner_of(slab, step, slabs) for step in range(1, slabs)]
    for partner in partners:

        @pl.when(partner < slab)
        def _():
            pl.semaphore_signal(barrier, inc=1, device_id=(energy, partner), device_id_type=MESH)

    for step in range(1, energies):
        pl.semaphore_signal(
            barrier, inc=1, device_id=(partner_of(energy, step, energies), slab), device_id_type=MESH
        )
    load_decay.wait()
    decays[slab] = jnp.broadcast_to(decay_ref[...], (POWERS, width))

    load_hamilton.wait()
    h1 = hamilton[...]
    t1 = h1.T
    h1s, t1s = split(h1), split(t1)
    h2 = mul(h1s, h1s)
    t2 = mul(t1s, t1s)
    h2s, t2s = split(h2), split(t2)
    h4 = mul(h2s, h2s)
    t3 = mul(t2s, t1s)
    square[...] = h2

    def trace(product):
        return jnp.sum(product, axis=0, keepdims=True)

    eye = lax.broadcasted_iota(jnp.int32, h1.shape, 0) == lax.broadcasted_iota(jnp.int32, h1.shape, 1)
    diagonals = jnp.concatenate(
        [
            jnp.ones((1, width), jnp.float32),
            trace(jnp.where(eye, h1, 0.0)),
            trace(t1 * h1),
            trace(t1 * h2),
            trace(t2 * h2),
            trace(t1 * h4),
            trace(t2 * h4),
            trace(t3 * h4),
        ],
        axis=0,
    )
    load_coupling.wait()
    terms[slab] = diagonals * (coupling_ref[...] / slabs)

    pl.semaphore_wait(barrier, slabs - 1 - slab + energies - 1)

    def gathers(step):
        return [
            pltpu.make_async_remote_copy(
                src_ref=held.at[slab], dst_ref=held.at[slab], send_sem=send.at[step], recv_sem=recv.at[step],
                device_id=(energy, partners[step - 1]), device_id_type=MESH,
            )
            for held, send, recv in ((terms, term_send, term_recv), (decays, decay_send, decay_recv))
        ]

    for step in range(1, slabs):

        @pl.when(partners[step - 1] > slab)
        def _():
            for copy in gathers(step):
                copy.start()

    h4s = split(h4)
    load_rows.wait()
    lane = lax.broadcasted_iota(jnp.int32, (1, width), 1)
    chosen = [rows_ref[0, energy * lines + line] for line in range(lines)]
    v0 = jnp.concatenate([(lane == row).astype(jnp.float32) for row in chosen], axis=0)
    v1 = jnp.concatenate([hamilton[pl.ds(row, 1), :] for row in chosen], axis=0)
    v2 = jnp.concatenate([square[pl.ds(row, 1), :] for row in chosen], axis=0)
    v3 = mul(split(v1), h2s)
    lower = jnp.concatenate([v0, v1, v2, v3], axis=0)
    upper = mul(split(lower), h4s)
    v = [lower[p * lines:(p + 1) * lines] for p in range(4)] + [upper[p * lines:(p + 1) * lines] for p in range(4)]
    inverses = [1.0 / (1.0 + k / total) for k in range(total)]
    picked = []
    for inverse in inverses:
        value = v[POWERS - 1]
        for p in reversed(range(POWERS - 1)):
            value = value * inverse + v[p]
        picked.append(value * inverse)

    for step in range(1, slabs):

        @pl.when(partners[step - 1] < slab)
        def _():
            for copy in gathers(step):
                copy.wait_recv()

    carried = jnp.zeros((POWERS, width), jnp.float32)
    for place in range(slabs - 1):
        carried = jnp.where(place < slab, decays[place] * carried + terms[place], carried)
    entering = []
    inverse_rows = 1.0 / (1.0 + lax.broadcasted_iota(jnp.int32, (total, width), 0).astype(jnp.float32) / total)
    incoming = jnp.broadcast_to(carried[POWERS - 1:], (total, width))
    for p in reversed(range(POWERS - 1)):
        incoming = incoming * inverse_rows + carried[p:p + 1]
    incoming = incoming * inverse_rows
    for k in range(total):
        entering.append(picked[k] * incoming[k:k + 1])
    u = jnp.concatenate(entering, axis=0)
    scale = 1.0 / (
        1.0 + (lax.broadcasted_iota(jnp.int32, u.shape, 0) // lines).astype(jnp.float32) / total
    )
    u = u + scale * mul(split(u), h1s)
    scale2 = scale * scale
    u = u + scale2 * mul(split(u), h2s)
    u = u + (scale2 * scale2) * mul(split(u), h4s)
    u = (jnp.concatenate(picked, axis=0) + scale * u).reshape(total, lines, width)
    dressed[pl.ds(0, total)] = u
    dressed[pl.ds(total, total)] = u

    load_screen.wait()

    def convolve(place):
        first = place * share

        def add(m, acc):
            return acc + dressed[pl.ds(total + first - m, share)] * screen[m][None]

        return lax.fori_loop(0, total, add, jnp.zeros((share, lines, width), jnp.float32), unroll=4)

    mine = pl.ds(pl.multiple_of(energy * lines, SUBLANES), lines)
    order = sorted(range(1, energies), key=lambda step: (step < energies // 2, step))
    sends = []
    for step in order:
        place = partner_of(energy, step, energies)
        sigma[step] = convolve(place)
        copy = pltpu.make_async_remote_copy(
            src_ref=sigma.at[step], dst_ref=out_ref.at[:, mine, :],
            send_sem=sigma_send.at[step], recv_sem=sigma_recv.at[step],
            device_id=(place, slab), device_id_type=MESH,
        )
        copy.start()
        sends.append(copy)
    sigma[0] = convolve(energy)
    own = pltpu.make_async_copy(sigma.at[0], out_ref.at[:, mine, :], own_sem)
    own.start()
    for copy in sends:
        copy.wait()
    own.wait()
    for step in range(1, slabs):

        @pl.when(partners[step - 1] > slab)
        def _():
            for copy in gathers(step):
                copy.wait_send()


def fused(energies, slabs, hamiltonian, decay, coupling, rows, screened):
    total, lines, width = screened.shape
    share = total // energies
    dma = pltpu.SemaphoreType.DMA
    return pl.pallas_call(
        functools.partial(kernel, energies, slabs),
        out_shape=jax.ShapeDtypeStruct((share, lines * energies, width), jnp.float32),
        in_specs=[pl.BlockSpec(memory_space=pltpu.HBM)] * 5,
        out_specs=pl.BlockSpec(memory_space=pl.ANY),
        scratch_shapes=[
            pltpu.SMEM(rows.shape, jnp.int32),
            pltpu.VMEM(decay.shape, jnp.float32),
            pltpu.VMEM(coupling.shape, jnp.float32),
            pltpu.VMEM((width, width), jnp.float32),
            pltpu.VMEM((width, width), jnp.float32),
            pltpu.VMEM((total, lines, width), jnp.float32),
            pltpu.VMEM((2 * total, lines, width), jnp.float32),
            pltpu.VMEM((energies, share, lines, width), jnp.float32),
            pltpu.VMEM((slabs, POWERS, width), jnp.float32),
            pltpu.VMEM((slabs, POWERS, width), jnp.float32),
            dma((5,)),
            dma((slabs,)),
            dma((slabs,)),
            dma((slabs,)),
            dma((slabs,)),
            dma((energies,)),
            dma((energies,)),
            dma,
        ],
        compiler_params=pltpu.CompilerParams(
            collective_id=0, has_side_effects=True, vmem_limit_bytes=60 * 1024 * 1024
        ),
    )(rows, decay, coupling, hamiltonian, screened)


def unfused(energies, slabs, hamiltonian, decay, coupling, rows, screened):
    total, lines, width = screened.shape
    share = total // energies
    dot = functools.partial(jnp.dot, precision=lax.Precision.HIGHEST)
    powers = [jnp.eye(width, dtype=jnp.float32)]
    for _ in range(POWERS - 1):
        powers.append(dot(powers[-1], hamiltonian))
    powers = jnp.stack(powers)
    own = coupling * jnp.diagonal(powers, axis1=1, axis2=2) / slabs
    decays = lax.all_gather(decay, "slab", axis=0, tiled=True)
    terms = lax.all_gather(own[None], "slab", axis=0, tiled=True)
    slab = lax.axis_index("slab")

    def advance(place, carried):
        return jnp.where(place < slab, decays[place] * carried + terms[place], carried)

    carried = lax.fori_loop(0, slabs - 1, advance, jnp.zeros_like(own))
    shifts = 1.0 + jnp.arange(total, dtype=jnp.int32).astype(jnp.float32) / total
    weights = shifts[:, None] ** -(1.0 + jnp.arange(POWERS, dtype=jnp.float32))
    incoming = dot(weights, carried)
    chosen = lax.dynamic_slice_in_dim(rows[0], lax.axis_index("energy") * lines, lines)
    picked = jnp.einsum("kp,prj->krj", weights, jnp.take(powers, chosen, axis=1), precision=lax.Precision.HIGHEST)
    scale = 1.0 / shifts[:, None, None]
    u = picked * incoming[:, None, :]
    u = u + scale * dot(u, powers[1])
    u = u + scale**2 * dot(u, powers[2])
    u = u + scale**4 * dot(u, powers[4])
    dressed = picked + scale * u

    def convolve(m, acc):
        return acc + jnp.roll(dressed, m, axis=0) * screened[m][None]

    sigma = lax.fori_loop(0, total, convolve, jnp.zeros_like(dressed))
    return lax.all_to_all(sigma, "energy", split_axis=0, concat_axis=1, tiled=True)


def solution(mesh):
    energies, slabs = mesh.shape["energy"], mesh.shape["slab"]

    def shards(hamiltonian, decay, coupling, rows, screened):
        lines = screened.shape[2]
        fits = lines % SUBLANES == 0 and all(count & (count - 1) == 0 for count in (energies, slabs))
        form = fused if fits else unfused
        return form(energies, slabs, hamiltonian, decay, coupling, rows, screened[0])

    in_specs = (
        P("slab", None),
        P("slab", None),
        P("slab", None),
        P("slab", None),
        P("slab", None, "energy", None),
    )
    out_specs = P("energy", "slab", None)
    return jax.shard_map(shards, mesh=mesh, in_specs=in_specs, out_specs=out_specs, check_vma=False)
```

```python
import functools

import jax
import jax.numpy as jnp
from jax import lax
from jax.experimental import pallas as pl
from jax.experimental.pallas import tpu as pltpu
from jax.sharding import PartitionSpec as P

MESH = pl.DeviceIdType.MESH
POWERS = 8
SUBLANES = 8


def split(a):
    high = a.astype(jnp.bfloat16)
    return high, (a - high.astype(jnp.float32)).astype(jnp.bfloat16)


def mul(a, b):
    (a_high, a_low), (b_high, b_low) = a, b
    dot = functools.partial(jnp.dot, preferred_element_type=jnp.float32)
    return dot(a_high, b_high) + (dot(a_high, b_low) + dot(a_low, b_high))


def partner_of(place, step, count):
    bit = 1
    while bit <= step:
        if step & bit:
            place = place + bit - 2 * bit * lax.rem(lax.div(place, bit), 2)
        bit *= 2
    return place


def kernel(
    energies, slabs, rows_hbm, decay_hbm, coupling_hbm, hamilton_ref, screened_ref, out_ref,
    rows_ref, decay_ref, coupling_ref, hamilton, square, screen, dressed, sigma, decays, terms,
    in_sem, decay_send, decay_recv, term_send, term_recv, sigma_send, sigma_recv,
):
    energy, slab = lax.axis_index("energy"), lax.axis_index("slab")
    total, lines, width = screen.shape
    share = total // energies

    loads = [
        pltpu.make_async_copy(source, held, in_sem.at[place])
        for place, (source, held) in enumerate(
            [
                (hamilton_ref, hamilton),
                (coupling_hbm, coupling_ref),
                (decay_hbm, decay_ref),
                (rows_hbm, rows_ref),
                (screened_ref, screen),
            ]
        )
    ]
    for load in loads:
        load.start()
    load_hamilton, load_coupling, load_decay, load_rows, load_screen = loads

    barrier = pltpu.get_barrier_semaphore()
    partners = [partner_of(slab, step, slabs) for step in range(1, slabs)]
    for partner in partners:

        @pl.when(partner < slab)
        def _():
            pl.semaphore_signal(barrier, inc=1, device_id=(energy, partner), device_id_type=MESH)

    for step in range(1, energies):
        pl.semaphore_signal(
            barrier, inc=1, device_id=(partner_of(energy, step, energies), slab), device_id_type=MESH
        )
    load_decay.wait()
    decays[slab] = jnp.broadcast_to(decay_ref[...], (POWERS, width))

    load_hamilton.wait()
    h1 = hamilton[...]
    t1 = h1.T
    h1s, t1s = split(h1), split(t1)
    h2 = mul(h1s, h1s)
    t2 = mul(t1s, t1s)
    h2s, t2s = split(h2), split(t2)
    h4 = mul(h2s, h2s)
    t3 = mul(t2s, t1s)
    square[...] = h2

    def trace(product):
        return jnp.sum(product, axis=0, keepdims=True)

    eye = lax.broadcasted_iota(jnp.int32, h1.shape, 0) == lax.broadcasted_iota(jnp.int32, h1.shape, 1)
    diagonals = jnp.concatenate(
        [
            jnp.ones((1, width), jnp.float32),
            trace(jnp.where(eye, h1, 0.0)),
            trace(t1 * h1),
            trace(t1 * h2),
            trace(t2 * h2),
            trace(t1 * h4),
            trace(t2 * h4),
            trace(t3 * h4),
        ],
        axis=0,
    )
    load_coupling.wait()
    terms[slab] = diagonals * (coupling_ref[...] / slabs)

    pl.semaphore_wait(barrier, slabs - 1 - slab + energies - 1)

    def gathers(step):
        return [
            pltpu.make_async_remote_copy(
                src_ref=held.at[slab, taken], dst_ref=held.at[slab, taken], send_sem=send.at[step], recv_sem=recv.at[step],
                device_id=(energy, partners[step - 1]), device_id_type=MESH,
            )
            for held, taken, send, recv in (
                (terms, pl.ds(0, POWERS), term_send, term_recv),
                (decays, pl.ds(0, 1), decay_send, decay_recv),
            )
        ]

    for step in range(1, slabs):

        @pl.when(partners[step - 1] > slab)
        def _():
            for copy in gathers(step):
                copy.start()

    h4s = split(h4)
    load_rows.wait()
    lane = lax.broadcasted_iota(jnp.int32, (1, width), 1)
    chosen = [rows_ref[0, energy * lines + line] for line in range(lines)]
    v0 = jnp.concatenate([(lane == row).astype(jnp.float32) for row in chosen], axis=0)
    v1 = jnp.concatenate([hamilton[pl.ds(row, 1), :] for row in chosen], axis=0)
    v2 = jnp.concatenate([square[pl.ds(row, 1), :] for row in chosen], axis=0)
    v3 = mul(split(v1), h2s)
    lower = jnp.concatenate([v0, v1, v2, v3], axis=0)
    upper = mul(split(lower), h4s)
    v = [lower[p * lines:(p + 1) * lines] for p in range(4)] + [upper[p * lines:(p + 1) * lines] for p in range(4)]
    inverses = [1.0 / (1.0 + k / total) for k in range(total)]
    picked = []
    for inverse in inverses:
        value = v[POWERS - 1]
        for p in reversed(range(POWERS - 1)):
            value = value * inverse + v[p]
        picked.append(value * inverse)

    for step in range(1, slabs):

        @pl.when(partners[step - 1] < slab)
        def _():
            for copy in gathers(step):
                copy.wait_recv()

    carried = jnp.zeros((POWERS, width), jnp.float32)
    for place in range(slabs - 1):
        carried = jnp.where(place < slab, decays[place, 0:1] * carried + terms[place], carried)
    entering = []
    inverse_rows = 1.0 / (1.0 + lax.broadcasted_iota(jnp.int32, (total, width), 0).astype(jnp.float32) / total)
    incoming = jnp.broadcast_to(carried[POWERS - 1:], (total, width))
    for p in reversed(range(POWERS - 1)):
        incoming = incoming * inverse_rows + carried[p:p + 1]
    incoming = incoming * inverse_rows
    for k in range(total):
        entering.append(picked[k] * incoming[k:k + 1])
    u = jnp.concatenate(entering, axis=0)
    scale = 1.0 / (
        1.0 + (lax.broadcasted_iota(jnp.int32, u.shape, 0) // lines).astype(jnp.float32) / total
    )
    u = u + scale * mul(split(u), h1s)
    scale2 = scale * scale
    u = u + scale2 * mul(split(u), h2s)
    u = u + (scale2 * scale2) * mul(split(u), h4s)
    u = (jnp.concatenate(picked, axis=0) + scale * u).reshape(total, lines, width)
    dressed[pl.ds(0, total)] = u
    dressed[pl.ds(total, total)] = u

    load_screen.wait()

    def convolve(place):
        first = place * share

        def add(m, acc):
            return acc + dressed[pl.ds(total + first - m, share)] * screen[m][None]

        return lax.fori_loop(0, total, add, jnp.zeros((share, lines, width), jnp.float32), unroll=4)

    mine = pl.ds(pl.multiple_of(energy * lines, SUBLANES), lines)
    order = sorted(range(1, energies), key=lambda step: (step < energies // 2, step))
    sends = []
    for step in order:
        place = partner_of(energy, step, energies)
        sigma[step] = convolve(place)
        copy = pltpu.make_async_remote_copy(
            src_ref=sigma.at[step], dst_ref=out_ref.at[:, mine, :],
            send_sem=sigma_send.at[step], recv_sem=sigma_recv.at[step],
            device_id=(place, slab), device_id_type=MESH,
        )
        copy.start()
        sends.append(copy)
    out_ref[:, mine, :] = convolve(energy)
    for copy in sends:
        copy.wait()
    for step in range(1, slabs):

        @pl.when(partners[step - 1] > slab)
        def _():
            for copy in gathers(step):
                copy.wait_send()


def fused(energies, slabs, hamiltonian, decay, coupling, rows, screened):
    total, lines, width = screened.shape
    share = total // energies
    dma = pltpu.SemaphoreType.DMA
    return pl.pallas_call(
        functools.partial(kernel, energies, slabs),
        out_shape=pltpu.VMEM((share, lines * energies, width), jnp.float32),
        in_specs=[pl.BlockSpec(memory_space=pltpu.HBM)] * 5,
        out_specs=pl.BlockSpec(memory_space=pltpu.VMEM),
        scratch_shapes=[
            pltpu.SMEM(rows.shape, jnp.int32),
            pltpu.VMEM(decay.shape, jnp.float32),
            pltpu.VMEM(coupling.shape, jnp.float32),
            pltpu.VMEM((width, width), jnp.float32),
            pltpu.VMEM((width, width), jnp.float32),
            pltpu.VMEM((total, lines, width), jnp.float32),
            pltpu.VMEM((2 * total, lines, width), jnp.float32),
            pltpu.VMEM((energies, share, lines, width), jnp.float32),
            pltpu.VMEM((slabs, POWERS, width), jnp.float32),
            pltpu.VMEM((slabs, POWERS, width), jnp.float32),
            dma((5,)),
            dma((slabs,)),
            dma((slabs,)),
            dma((slabs,)),
            dma((slabs,)),
            dma((energies,)),
            dma((energies,)),
        ],
        compiler_params=pltpu.CompilerParams(
            collective_id=0, has_side_effects=True, vmem_limit_bytes=60 * 1024 * 1024
        ),
    )(rows, decay, coupling, hamiltonian, screened)


def unfused(energies, slabs, hamiltonian, decay, coupling, rows, screened):
    total, lines, width = screened.shape
    share = total // energies
    dot = functools.partial(jnp.dot, precision=lax.Precision.HIGHEST)
    powers = [jnp.eye(width, dtype=jnp.float32)]
    for _ in range(POWERS - 1):
        powers.append(dot(powers[-1], hamiltonian))
    powers = jnp.stack(powers)
    own = coupling * jnp.diagonal(powers, axis1=1, axis2=2) / slabs
    decays = lax.all_gather(decay, "slab", axis=0, tiled=True)
    terms = lax.all_gather(own[None], "slab", axis=0, tiled=True)
    slab = lax.axis_index("slab")

    def advance(place, carried):
        return jnp.where(place < slab, decays[place] * carried + terms[place], carried)

    carried = lax.fori_loop(0, slabs - 1, advance, jnp.zeros_like(own))
    shifts = 1.0 + jnp.arange(total, dtype=jnp.int32).astype(jnp.float32) / total
    weights = shifts[:, None] ** -(1.0 + jnp.arange(POWERS, dtype=jnp.float32))
    incoming = dot(weights, carried)
    chosen = lax.dynamic_slice_in_dim(rows[0], lax.axis_index("energy") * lines, lines)
    picked = jnp.einsum("kp,prj->krj", weights, jnp.take(powers, chosen, axis=1), precision=lax.Precision.HIGHEST)
    scale = 1.0 / shifts[:, None, None]
    u = picked * incoming[:, None, :]
    u = u + scale * dot(u, powers[1])
    u = u + scale**2 * dot(u, powers[2])
    u = u + scale**4 * dot(u, powers[4])
    dressed = picked + scale * u

    def convolve(m, acc):
        return acc + jnp.roll(dressed, m, axis=0) * screened[m][None]

    sigma = lax.fori_loop(0, total, convolve, jnp.zeros_like(dressed))
    return lax.all_to_all(sigma, "energy", split_axis=0, concat_axis=1, tiled=True)


def solution(mesh):
    energies, slabs = mesh.shape["energy"], mesh.shape["slab"]

    def shards(hamiltonian, decay, coupling, rows, screened):
        lines = screened.shape[2]
        fits = lines % SUBLANES == 0 and all(count & (count - 1) == 0 for count in (energies, slabs))
        form = fused if fits else unfused
        return form(energies, slabs, hamiltonian, decay, coupling, rows, screened[0])

    in_specs = (
        P("slab", None),
        P("slab", None),
        P("slab", None),
        P("slab", None),
        P("slab", None, "energy", None),
    )
    out_specs = P("energy", "slab", None)
    return jax.shard_map(shards, mesh=mesh, in_specs=in_specs, out_specs=out_specs, check_vma=False)
```

```python
import functools

import jax
import jax.numpy as jnp
from jax import lax
from jax.experimental import pallas as pl
from jax.experimental.pallas import tpu as pltpu
from jax.sharding import PartitionSpec as P

MESH = pl.DeviceIdType.MESH
POWERS = 8
SUBLANES = 8
EARLY = 1


def split(a):
    high = a.astype(jnp.bfloat16)
    return high, (a - high.astype(jnp.float32)).astype(jnp.bfloat16)


def mul(a, b):
    (a_high, a_low), (b_high, b_low) = a, b
    dot = functools.partial(jnp.dot, preferred_element_type=jnp.float32)
    return dot(a_high, b_high) + (dot(a_high, b_low) + dot(a_low, b_high))


def partner_of(place, step, count):
    bit = 1
    while bit <= step:
        if step & bit:
            place = place + bit - 2 * bit * lax.rem(lax.div(place, bit), 2)
        bit *= 2
    return place


def kernel(
    energies, slabs, rows_hbm, decay_hbm, coupling_hbm, hamilton_ref, screened_ref, out_ref,
    rows_ref, decay_ref, coupling_ref, hamilton, square, screen, early, dressed, sigma, arrived, decays, terms,
    in_sem, decay_send, decay_recv, term_send, term_recv, sigma_send, sigma_recv, early_send, early_recv,
):
    energy, slab = lax.axis_index("energy"), lax.axis_index("slab")
    total, lines, width = screen.shape
    share = total // energies

    loads = [
        pltpu.make_async_copy(source, held, in_sem.at[place])
        for place, (source, held) in enumerate(
            [
                (hamilton_ref, hamilton),
                (coupling_hbm, coupling_ref),
                (decay_hbm, decay_ref),
                (rows_hbm, rows_ref),
                (screened_ref, screen),
            ]
        )
    ]
    for load in loads:
        load.start()
    load_hamilton, load_coupling, load_decay, load_rows, load_screen = loads

    barrier = pltpu.get_barrier_semaphore()
    partners = [partner_of(slab, step, slabs) for step in range(1, slabs)]
    for partner in partners:

        @pl.when(partner < slab)
        def _():
            pl.semaphore_signal(barrier, inc=1, device_id=(energy, partner), device_id_type=MESH)

    for step in range(1, energies):
        pl.semaphore_signal(
            barrier, inc=1, device_id=(partner_of(energy, step, energies), slab), device_id_type=MESH
        )
    load_decay.wait()
    decays[slab] = jnp.broadcast_to(decay_ref[...], (POWERS, width))

    load_hamilton.wait()
    h1 = hamilton[...]
    t1 = h1.T
    h1s, t1s = split(h1), split(t1)
    h2 = mul(h1s, h1s)
    t2 = mul(t1s, t1s)
    h2s, t2s = split(h2), split(t2)
    h4 = mul(h2s, h2s)
    t3 = mul(t2s, t1s)
    square[...] = h2

    def trace(product):
        return jnp.sum(product, axis=0, keepdims=True)

    eye = lax.broadcasted_iota(jnp.int32, h1.shape, 0) == lax.broadcasted_iota(jnp.int32, h1.shape, 1)
    diagonals = jnp.concatenate(
        [
            jnp.ones((1, width), jnp.float32),
            trace(jnp.where(eye, h1, 0.0)),
            trace(t1 * h1),
            trace(t1 * h2),
            trace(t2 * h2),
            trace(t1 * h4),
            trace(t2 * h4),
            trace(t3 * h4),
        ],
        axis=0,
    )
    load_coupling.wait()
    terms[slab] = diagonals * (coupling_ref[...] / slabs)

    pl.semaphore_wait(barrier, slabs - 1 - slab + energies - 1)

    def gathers(step):
        return [
            pltpu.make_async_remote_copy(
                src_ref=held.at[slab, taken], dst_ref=held.at[slab, taken], send_sem=send.at[step], recv_sem=recv.at[step],
                device_id=(energy, partners[step - 1]), device_id_type=MESH,
            )
            for held, taken, send, recv in (
                (terms, pl.ds(0, POWERS), term_send, term_recv),
                (decays, pl.ds(0, 1), decay_send, decay_recv),
            )
        ]

    for step in range(1, slabs):

        @pl.when(partners[step - 1] > slab)
        def _():
            for copy in gathers(step):
                copy.start()

    kept = lines - EARLY
    shares = []
    for step in range(1, energies):
        copy = pltpu.make_async_remote_copy(
            src_ref=screened_ref.at[:, pl.ds(kept, EARLY), :], dst_ref=early.at[energy, :, pl.ds(kept, EARLY), :],
            send_sem=early_send.at[step], recv_sem=early_recv.at[step],
            device_id=(partner_of(energy, step, energies), slab), device_id_type=MESH,
        )
        copy.start()
        shares.append(copy)

    h4s = split(h4)
    lane = lax.broadcasted_iota(jnp.int32, (1, width), 1)
    inverses = [1.0 / (1.0 + k / total) for k in range(total)]
    load_rows.wait()

    def pick(places):
        chosen = [rows_ref[0, place] for place in places]
        v0 = jnp.concatenate([(lane == row).astype(jnp.float32) for row in chosen], axis=0)
        v1 = jnp.concatenate([hamilton[pl.ds(row, 1), :] for row in chosen], axis=0)
        v2 = jnp.concatenate([square[pl.ds(row, 1), :] for row in chosen], axis=0)
        v3 = mul(split(v1), h2s)
        lower = jnp.concatenate([v0, v1, v2, v3], axis=0)
        upper = mul(split(lower), h4s)
        v = [part[p * lines:(p + 1) * lines] for part in (lower, upper) for p in range(POWERS // 2)]
        picked = []
        for inverse in inverses:
            value = v[POWERS - 1]
            for p in reversed(range(POWERS - 1)):
                value = value * inverse + v[p]
            picked.append(value * inverse)
        return picked

    picked = pick([energy * lines + line for line in range(lines)])

    for step in range(1, slabs):

        @pl.when(partners[step - 1] < slab)
        def _():
            for copy in gathers(step):
                copy.wait_recv()

    carried = jnp.zeros((POWERS, width), jnp.float32)
    for place in range(slabs - 1):
        carried = jnp.where(place < slab, decays[place, 0:1] * carried + terms[place], carried)
    inverse_rows = 1.0 / (1.0 + lax.broadcasted_iota(jnp.int32, (total, width), 0).astype(jnp.float32) / total)
    incoming = jnp.broadcast_to(carried[POWERS - 1:], (total, width))
    for p in reversed(range(POWERS - 1)):
        incoming = incoming * inverse_rows + carried[p:p + 1]
    incoming = incoming * inverse_rows
    scale = 1.0 / (
        1.0 + (lax.broadcasted_iota(jnp.int32, (total * lines, width), 0) // lines).astype(jnp.float32) / total
    )
    scale2 = scale * scale

    def dress(picked):
        u = jnp.concatenate([picked[k] * incoming[k:k + 1] for k in range(total)], axis=0)
        u = u + scale * mul(split(u), h1s)
        u = u + scale2 * mul(split(u), h2s)
        u = u + (scale2 * scale2) * mul(split(u), h4s)
        u = (jnp.concatenate(picked, axis=0) + scale * u).reshape(total, lines, width)
        dressed[pl.ds(0, total)] = u
        dressed[pl.ds(total, total)] = u

    def convolve(place, held):
        first = place * share

        def add(m, acc):
            return acc + dressed[pl.ds(total + first - m, share)] * held[m][None]

        return lax.fori_loop(0, total, add, jnp.zeros((share, lines, width), jnp.float32), unroll=4)

    dress(picked)
    load_screen.wait()

    def pack(block):
        fill = jnp.concatenate(
            [jnp.zeros((kept, kept, width), jnp.float32)] + [block[k, :kept][:, None] for k in range(kept, share)], axis=1
        )
        line = lax.broadcasted_iota(jnp.int32, fill.shape, 1)
        return jnp.where(line < kept, block[:kept], fill)

    order = sorted(range(1, energies), key=lambda step: (step < energies // 2, step))
    sends = []
    for step in order:
        place = partner_of(energy, step, energies)
        sigma[step] = pack(convolve(place, screen))
        copy = pltpu.make_async_remote_copy(
            src_ref=sigma.at[step], dst_ref=arrived.at[energy],
            send_sem=sigma_send.at[step], recv_sem=sigma_recv.at[step],
            device_id=(place, slab), device_id_type=MESH,
        )
        copy.start()
        sends.append(copy)
    arrived[energy] = pack(convolve(energy, screen))

    places = [place * lines + kept + line for place in range(energies) for line in range(EARLY)]
    dress(pick(places + [places[-1]] * (lines - len(places))))
    early[energy, :, pl.ds(kept, EARLY), :] = screen[:, kept:]
    for copy in shares:
        copy.wait()
    parts = [early[place, :, pl.ds(kept, EARLY), :] for place in range(energies)]
    parts += [jnp.zeros((total, lines - len(places), width), jnp.float32)] * (len(places) < lines)
    screen[...] = jnp.concatenate(parts, axis=1)
    result = convolve(energy, screen)
    for place in range(energies):
        out_ref[:, pl.ds(place * lines + kept, EARLY), :] = result[:, place * EARLY:(place + 1) * EARLY]

    for copy in sends:
        copy.wait()
    for place in range(energies):
        first = place * lines
        out_ref[:kept, first:first + kept] = arrived[place, :, :kept]
        for k in range(kept, share):
            out_ref[k, first:first + kept] = arrived[place, :, k]
    for step in range(1, slabs):

        @pl.when(partners[step - 1] > slab)
        def _():
            for copy in gathers(step):
                copy.wait_send()


def fused(energies, slabs, hamiltonian, decay, coupling, rows, screened):
    total, lines, width = screened.shape
    share = total // energies
    dma = pltpu.SemaphoreType.DMA
    return pl.pallas_call(
        functools.partial(kernel, energies, slabs),
        out_shape=pltpu.VMEM((share, lines * energies, width), jnp.float32),
        in_specs=[pl.BlockSpec(memory_space=pltpu.HBM)] * 5,
        out_specs=pl.BlockSpec(memory_space=pltpu.VMEM),
        scratch_shapes=[
            pltpu.SMEM(rows.shape, jnp.int32),
            pltpu.VMEM(decay.shape, jnp.float32),
            pltpu.VMEM(coupling.shape, jnp.float32),
            pltpu.VMEM((width, width), jnp.float32),
            pltpu.VMEM((width, width), jnp.float32),
            pltpu.VMEM((total, lines, width), jnp.float32),
            pltpu.VMEM((energies, total, lines, width), jnp.float32),
            pltpu.VMEM((2 * total, lines, width), jnp.float32),
            pltpu.VMEM((energies, share - EARLY, lines, width), jnp.float32),
            pltpu.VMEM((energies, share - EARLY, lines, width), jnp.float32),
            pltpu.VMEM((slabs, POWERS, width), jnp.float32),
            pltpu.VMEM((slabs, POWERS, width), jnp.float32),
            dma((5,)),
            dma((slabs,)),
            dma((slabs,)),
            dma((slabs,)),
            dma((slabs,)),
            dma((energies,)),
            dma((energies,)),
            dma((energies,)),
            dma((energies,)),
        ],
        compiler_params=pltpu.CompilerParams(
            collective_id=0, has_side_effects=True, vmem_limit_bytes=60 * 1024 * 1024
        ),
    )(rows, decay, coupling, hamiltonian, screened)


def unfused(energies, slabs, hamiltonian, decay, coupling, rows, screened):
    total, lines, width = screened.shape
    share = total // energies
    dot = functools.partial(jnp.dot, precision=lax.Precision.HIGHEST)
    powers = [jnp.eye(width, dtype=jnp.float32)]
    for _ in range(POWERS - 1):
        powers.append(dot(powers[-1], hamiltonian))
    powers = jnp.stack(powers)
    own = coupling * jnp.diagonal(powers, axis1=1, axis2=2) / slabs
    decays = lax.all_gather(decay, "slab", axis=0, tiled=True)
    terms = lax.all_gather(own[None], "slab", axis=0, tiled=True)
    slab = lax.axis_index("slab")

    def advance(place, carried):
        return jnp.where(place < slab, decays[place] * carried + terms[place], carried)

    carried = lax.fori_loop(0, slabs - 1, advance, jnp.zeros_like(own))
    shifts = 1.0 + jnp.arange(total, dtype=jnp.int32).astype(jnp.float32) / total
    weights = shifts[:, None] ** -(1.0 + jnp.arange(POWERS, dtype=jnp.float32))
    incoming = dot(weights, carried)
    chosen = lax.dynamic_slice_in_dim(rows[0], lax.axis_index("energy") * lines, lines)
    picked = jnp.einsum("kp,prj->krj", weights, jnp.take(powers, chosen, axis=1), precision=lax.Precision.HIGHEST)
    scale = 1.0 / shifts[:, None, None]
    u = picked * incoming[:, None, :]
    u = u + scale * dot(u, powers[1])
    u = u + scale**2 * dot(u, powers[2])
    u = u + scale**4 * dot(u, powers[4])
    dressed = picked + scale * u

    def convolve(m, acc):
        return acc + jnp.roll(dressed, m, axis=0) * screened[m][None]

    sigma = lax.fori_loop(0, total, convolve, jnp.zeros_like(dressed))
    return lax.all_to_all(sigma, "energy", split_axis=0, concat_axis=1, tiled=True)


def solution(mesh):
    energies, slabs = mesh.shape["energy"], mesh.shape["slab"]

    def shards(hamiltonian, decay, coupling, rows, screened):
        lines = screened.shape[2]
        fits = lines == screened.shape[1] // energies == SUBLANES >= energies * EARLY and all(count & (count - 1) == 0 for count in (energies, slabs))
        form = fused if fits else unfused
        return form(energies, slabs, hamiltonian, decay, coupling, rows, screened[0])

    in_specs = (
        P("slab", None),
        P("slab", None),
        P("slab", None),
        P("slab", None),
        P("slab", None, "energy", None),
    )
    out_specs = P("energy", "slab", None)
    return jax.shard_map(shards, mesh=mesh, in_specs=in_specs, out_specs=out_specs, check_vma=False)
```

```python
import functools

import jax
import jax.numpy as jnp
from jax import lax
from jax.experimental import pallas as pl
from jax.experimental.pallas import tpu as pltpu
from jax.sharding import PartitionSpec as P

MESH = pl.DeviceIdType.MESH
POWERS = 8
SUBLANES = 8
EARLY = 1


def split(a):
    high = a.astype(jnp.bfloat16)
    return high, (a - high.astype(jnp.float32)).astype(jnp.bfloat16)


def mul(a, b):
    (a_high, a_low), (b_high, b_low) = a, b
    dot = functools.partial(jnp.dot, preferred_element_type=jnp.float32)
    return dot(a_high, b_high) + (dot(a_high, b_low) + dot(a_low, b_high))


def partner_of(place, step, count):
    bit = 1
    while bit <= step:
        if step & bit:
            place = place + bit - 2 * bit * lax.rem(lax.div(place, bit), 2)
        bit *= 2
    return place


def kernel(
    energies, slabs, rows_hbm, decay_hbm, coupling_hbm, hamilton_ref, screened_ref, out_ref,
    rows_ref, decay_ref, coupling_ref, hamilton, square, screen, early, dressed, sigma, arrived, decays, terms,
    in_sem, decay_send, decay_recv, term_send, term_recv, sigma_send, sigma_recv, early_send, early_recv,
):
    energy, slab = lax.axis_index("energy"), lax.axis_index("slab")
    total, lines, width = screen.shape
    share = total // energies

    loads = [
        pltpu.make_async_copy(source, held, in_sem.at[place])
        for place, (source, held) in enumerate(
            [
                (hamilton_ref, hamilton),
                (coupling_hbm, coupling_ref),
                (decay_hbm, decay_ref),
                (rows_hbm, rows_ref),
                (screened_ref, screen),
            ]
        )
    ]
    for load in loads:
        load.start()
    load_hamilton, load_coupling, load_decay, load_rows, load_screen = loads

    barrier = pltpu.get_barrier_semaphore()
    partners = [partner_of(slab, step, slabs) for step in range(1, slabs)]
    for partner in partners:

        @pl.when(partner < slab)
        def _():
            pl.semaphore_signal(barrier, inc=1, device_id=(energy, partner), device_id_type=MESH)

    for step in range(1, energies):
        pl.semaphore_signal(
            barrier, inc=1, device_id=(partner_of(energy, step, energies), slab), device_id_type=MESH
        )
    load_decay.wait()
    decays[slab] = jnp.broadcast_to(decay_ref[...], (POWERS, width))

    load_hamilton.wait()
    h1 = hamilton[...]
    t1 = h1.T
    h1s, t1s = split(h1), split(t1)
    h2 = mul(h1s, h1s)
    t2 = mul(t1s, t1s)
    h2s, t2s = split(h2), split(t2)
    h4 = mul(h2s, h2s)
    t3 = mul(t2s, t1s)
    square[...] = h2

    def trace(product):
        return jnp.sum(product, axis=0, keepdims=True)

    eye = lax.broadcasted_iota(jnp.int32, h1.shape, 0) == lax.broadcasted_iota(jnp.int32, h1.shape, 1)
    diagonals = jnp.concatenate(
        [
            jnp.ones((1, width), jnp.float32),
            trace(jnp.where(eye, h1, 0.0)),
            trace(t1 * h1),
            trace(t1 * h2),
            trace(t2 * h2),
            trace(t1 * h4),
            trace(t2 * h4),
            trace(t3 * h4),
        ],
        axis=0,
    )
    load_coupling.wait()
    terms[slab] = diagonals * (coupling_ref[...] / slabs)

    pl.semaphore_wait(barrier, slabs - 1 - slab + energies - 1)

    def gathers(step):
        return [
            pltpu.make_async_remote_copy(
                src_ref=held.at[slab, taken], dst_ref=held.at[slab, taken], send_sem=send.at[step], recv_sem=recv.at[step],
                device_id=(energy, partners[step - 1]), device_id_type=MESH,
            )
            for held, taken, send, recv in (
                (terms, pl.ds(0, POWERS), term_send, term_recv),
                (decays, pl.ds(0, 1), decay_send, decay_recv),
            )
        ]

    for step in range(1, slabs):

        @pl.when(partners[step - 1] > slab)
        def _():
            for copy in gathers(step):
                copy.start()

    kept = lines - EARLY
    shares = []
    for step in range(1, energies):
        copy = pltpu.make_async_remote_copy(
            src_ref=screened_ref.at[:, pl.ds(kept, EARLY), :], dst_ref=early.at[energy, :, pl.ds(kept, EARLY), :],
            send_sem=early_send.at[step], recv_sem=early_recv.at[step],
            device_id=(partner_of(energy, step, energies), slab), device_id_type=MESH,
        )
        copy.start()
        shares.append(copy)

    h4s = split(h4)
    lane = lax.broadcasted_iota(jnp.int32, (1, width), 1)
    inverses = [1.0 / (1.0 + k / total) for k in range(total)]
    load_rows.wait()

    def pick(places):
        chosen = [rows_ref[0, place] for place in places]
        v0 = jnp.concatenate([(lane == row).astype(jnp.float32) for row in chosen], axis=0)
        v1 = jnp.concatenate([hamilton[pl.ds(row, 1), :] for row in chosen], axis=0)
        v2 = jnp.concatenate([square[pl.ds(row, 1), :] for row in chosen], axis=0)
        v3 = mul(split(v1), h2s)
        lower = jnp.concatenate([v0, v1, v2, v3], axis=0)
        upper = mul(split(lower), h4s)
        v = [part[p * lines:(p + 1) * lines] for part in (lower, upper) for p in range(POWERS // 2)]
        picked = []
        for inverse in inverses:
            value = v[POWERS - 1]
            for p in reversed(range(POWERS - 1)):
                value = value * inverse + v[p]
            picked.append(value * inverse)
        return picked

    picked = pick([energy * lines + line for line in range(lines)])

    for step in range(1, slabs):

        @pl.when(partners[step - 1] < slab)
        def _():
            for copy in gathers(step):
                copy.wait_recv()

    carried = jnp.zeros((POWERS, width), jnp.float32)
    for place in range(slabs - 1):
        carried = jnp.where(place < slab, decays[place, 0:1] * carried + terms[place], carried)
    inverse_rows = 1.0 / (1.0 + lax.broadcasted_iota(jnp.int32, (total, width), 0).astype(jnp.float32) / total)
    incoming = jnp.broadcast_to(carried[POWERS - 1:], (total, width))
    for p in reversed(range(POWERS - 1)):
        incoming = incoming * inverse_rows + carried[p:p + 1]
    incoming = incoming * inverse_rows
    scale = 1.0 / (
        1.0 + (lax.broadcasted_iota(jnp.int32, (total * lines, width), 0) // lines).astype(jnp.float32) / total
    )
    scale2 = scale * scale

    def dress(picked):
        u = jnp.concatenate([picked[k] * incoming[k:k + 1] for k in range(total)], axis=0)
        u = u + scale * mul(split(u), h1s)
        u = u + scale2 * mul(split(u), h2s)
        u = u + (scale2 * scale2) * mul(split(u), h4s)
        u = (jnp.concatenate(picked, axis=0) + scale * u).reshape(total, lines, width)
        dressed[pl.ds(0, total)] = u
        dressed[pl.ds(total, total)] = u

    def convolve(place, held):
        first = place * share

        def add(m, acc):
            return acc + dressed[pl.ds(total + first - m, share)] * held[m][None]

        return lax.fori_loop(0, total, add, jnp.zeros((share, lines, width), jnp.float32), unroll=4)

    dress(picked)
    load_screen.wait()

    def pack(block):
        fill = jnp.concatenate(
            [jnp.zeros((kept, kept, width), jnp.float32)] + [block[k, :kept][:, None] for k in range(kept, share)], axis=1
        )
        line = lax.broadcasted_iota(jnp.int32, fill.shape, 1)
        return jnp.where(line < kept, block[:kept], fill)


    def deliver(slot, source, target):
        return pltpu.make_async_remote_copy(
            src_ref=sigma.at[slot], dst_ref=arrived.at[source],
            send_sem=sigma_send.at[slot], recv_sem=sigma_recv.at[source],
            device_id=(target, slab), device_id_type=MESH,
        )

    sends = []
    for slot in range(energies - 1):
        place = slot + (slot >= energy).astype(jnp.int32)
        sigma[slot] = pack(convolve(place, screen))
        copy = deliver(slot, energy, place)
        copy.start()
        sends.append(copy)
    arrived[energy] = pack(convolve(energy, screen))

    places = [place * lines + kept + line for place in range(energies) for line in range(EARLY)]
    dress(pick(places + [places[-1]] * (lines - len(places))))
    early[energy, :, pl.ds(kept, EARLY), :] = screen[:, kept:]
    for copy in shares:
        copy.wait()
    parts = [early[place, :, pl.ds(kept, EARLY), :] for place in range(energies)]
    parts += [jnp.zeros((total, lines - len(places), width), jnp.float32)] * (len(places) < lines)
    screen[...] = jnp.concatenate(parts, axis=1)
    result = convolve(energy, screen)
    for place in range(energies):
        out_ref[:, pl.ds(place * lines + kept, EARLY), :] = result[:, place * EARLY:(place + 1) * EARLY]

    for slot, copy in enumerate(sends):
        copy.wait_send()
        deliver(slot, slot + (slot >= energy).astype(jnp.int32), energy).wait_recv()
    for place in range(energies):
        first = place * lines
        out_ref[:kept, first:first + kept] = arrived[place, :, :kept]
        for k in range(kept, share):
            out_ref[k, first:first + kept] = arrived[place, :, k]
    for step in range(1, slabs):

        @pl.when(partners[step - 1] > slab)
        def _():
            for copy in gathers(step):
                copy.wait_send()


def fused(energies, slabs, hamiltonian, decay, coupling, rows, screened):
    total, lines, width = screened.shape
    share = total // energies
    dma = pltpu.SemaphoreType.DMA
    return pl.pallas_call(
        functools.partial(kernel, energies, slabs),
        out_shape=pltpu.VMEM((share, lines * energies, width), jnp.float32),
        in_specs=[pl.BlockSpec(memory_space=pltpu.HBM)] * 5,
        out_specs=pl.BlockSpec(memory_space=pltpu.VMEM),
        scratch_shapes=[
            pltpu.SMEM(rows.shape, jnp.int32),
            pltpu.VMEM(decay.shape, jnp.float32),
            pltpu.VMEM(coupling.shape, jnp.float32),
            pltpu.VMEM((width, width), jnp.float32),
            pltpu.VMEM((width, width), jnp.float32),
            pltpu.VMEM((total, lines, width), jnp.float32),
            pltpu.VMEM((energies, total, lines, width), jnp.float32),
            pltpu.VMEM((2 * total, lines, width), jnp.float32),
            pltpu.VMEM((energies, share - EARLY, lines, width), jnp.float32),
            pltpu.VMEM((energies, share - EARLY, lines, width), jnp.float32),
            pltpu.VMEM((slabs, POWERS, width), jnp.float32),
            pltpu.VMEM((slabs, POWERS, width), jnp.float32),
            dma((5,)),
            dma((slabs,)),
            dma((slabs,)),
            dma((slabs,)),
            dma((slabs,)),
            dma((energies,)),
            dma((energies,)),
            dma((energies,)),
            dma((energies,)),
        ],
        compiler_params=pltpu.CompilerParams(
            collective_id=0, has_side_effects=True, vmem_limit_bytes=60 * 1024 * 1024
        ),
    )(rows, decay, coupling, hamiltonian, screened)


def unfused(energies, slabs, hamiltonian, decay, coupling, rows, screened):
    total, lines, width = screened.shape
    share = total // energies
    dot = functools.partial(jnp.dot, precision=lax.Precision.HIGHEST)
    powers = [jnp.eye(width, dtype=jnp.float32)]
    for _ in range(POWERS - 1):
        powers.append(dot(powers[-1], hamiltonian))
    powers = jnp.stack(powers)
    own = coupling * jnp.diagonal(powers, axis1=1, axis2=2) / slabs
    decays = lax.all_gather(decay, "slab", axis=0, tiled=True)
    terms = lax.all_gather(own[None], "slab", axis=0, tiled=True)
    slab = lax.axis_index("slab")

    def advance(place, carried):
        return jnp.where(place < slab, decays[place] * carried + terms[place], carried)

    carried = lax.fori_loop(0, slabs - 1, advance, jnp.zeros_like(own))
    shifts = 1.0 + jnp.arange(total, dtype=jnp.int32).astype(jnp.float32) / total
    weights = shifts[:, None] ** -(1.0 + jnp.arange(POWERS, dtype=jnp.float32))
    incoming = dot(weights, carried)
    chosen = lax.dynamic_slice_in_dim(rows[0], lax.axis_index("energy") * lines, lines)
    picked = jnp.einsum("kp,prj->krj", weights, jnp.take(powers, chosen, axis=1), precision=lax.Precision.HIGHEST)
    scale = 1.0 / shifts[:, None, None]
    u = picked * incoming[:, None, :]
    u = u + scale * dot(u, powers[1])
    u = u + scale**2 * dot(u, powers[2])
    u = u + scale**4 * dot(u, powers[4])
    dressed = picked + scale * u

    def convolve(m, acc):
        return acc + jnp.roll(dressed, m, axis=0) * screened[m][None]

    sigma = lax.fori_loop(0, total, convolve, jnp.zeros_like(dressed))
    return lax.all_to_all(sigma, "energy", split_axis=0, concat_axis=1, tiled=True)


def solution(mesh):
    energies, slabs = mesh.shape["energy"], mesh.shape["slab"]

    def shards(hamiltonian, decay, coupling, rows, screened):
        lines = screened.shape[2]
        fits = lines == screened.shape[1] // energies == SUBLANES >= energies * EARLY and all(count & (count - 1) == 0 for count in (energies, slabs))
        form = fused if fits else unfused
        return form(energies, slabs, hamiltonian, decay, coupling, rows, screened[0])

    in_specs = (
        P("slab", None),
        P("slab", None),
        P("slab", None),
        P("slab", None),
        P("slab", None, "energy", None),
    )
    out_specs = P("energy", "slab", None)
    return jax.shard_map(shards, mesh=mesh, in_specs=in_specs, out_specs=out_specs, check_vma=False)
```

```python
import functools

import jax
import jax.numpy as jnp
from jax import lax
from jax.experimental import pallas as pl
from jax.experimental.pallas import tpu as pltpu
from jax.sharding import PartitionSpec as P

MESH = pl.DeviceIdType.MESH
POWERS = 8
SUBLANES = 8
EARLY = 1


def split(a):
    high = a.astype(jnp.bfloat16)
    return high, (a - high.astype(jnp.float32)).astype(jnp.bfloat16)


def mul(a, b):
    (a_high, a_low), (b_high, b_low) = a, b
    left = jnp.concatenate([a_low, a_high, a_high], axis=1)
    right = jnp.concatenate([b_high, b_low, b_high], axis=0)
    return jnp.dot(left, right, preferred_element_type=jnp.float32)


def partner_of(place, step, count):
    bit = 1
    while bit <= step:
        if step & bit:
            place = place + bit - 2 * bit * lax.rem(lax.div(place, bit), 2)
        bit *= 2
    return place


def kernel(
    energies, slabs, rows_hbm, decay_hbm, coupling_hbm, hamilton_ref, screened_ref, out_ref,
    rows_ref, decay_ref, coupling_ref, hamilton, square, screen, early, dressed, sigma, arrived, decays, terms,
    in_sem, decay_send, decay_recv, term_send, term_recv, sigma_send, sigma_recv, early_send, early_recv,
):
    energy, slab = lax.axis_index("energy"), lax.axis_index("slab")
    total, lines, width = screen.shape
    share = total // energies

    loads = [
        pltpu.make_async_copy(source, held, in_sem.at[place])
        for place, (source, held) in enumerate(
            [
                (hamilton_ref, hamilton),
                (coupling_hbm, coupling_ref),
                (decay_hbm, decay_ref),
                (rows_hbm, rows_ref),
                (screened_ref, screen),
            ]
        )
    ]
    for load in loads:
        load.start()
    load_hamilton, load_coupling, load_decay, load_rows, load_screen = loads

    barrier = pltpu.get_barrier_semaphore()
    partners = [partner_of(slab, step, slabs) for step in range(1, slabs)]
    for partner in partners:

        @pl.when(partner < slab)
        def _():
            pl.semaphore_signal(barrier, inc=1, device_id=(energy, partner), device_id_type=MESH)

    for step in range(1, energies):
        pl.semaphore_signal(
            barrier, inc=1, device_id=(partner_of(energy, step, energies), slab), device_id_type=MESH
        )
    load_decay.wait()
    decays[slab] = jnp.broadcast_to(decay_ref[...], (POWERS, width))

    load_hamilton.wait()
    h1 = hamilton[...]
    t1 = h1.T
    h1s, t1s = split(h1), split(t1)
    h2 = mul(h1s, h1s)
    t2 = h2.T
    h2s, t2s = split(h2), split(t2)
    h4 = mul(h2s, h2s)
    t3 = mul(t2s, t1s)
    square[...] = h2

    def trace(product):
        return jnp.sum(product, axis=0, keepdims=True)

    eye = lax.broadcasted_iota(jnp.int32, h1.shape, 0) == lax.broadcasted_iota(jnp.int32, h1.shape, 1)
    diagonals = jnp.concatenate(
        [
            jnp.ones((1, width), jnp.float32),
            trace(jnp.where(eye, h1, 0.0)),
            trace(t1 * h1),
            trace(t1 * h2),
            trace(t2 * h2),
            trace(t1 * h4),
            trace(t2 * h4),
            trace(t3 * h4),
        ],
        axis=0,
    )
    load_coupling.wait()
    terms[slab] = diagonals * (coupling_ref[...] / slabs)

    pl.semaphore_wait(barrier, slabs - 1 - slab + energies - 1)

    def gathers(step):
        return [
            pltpu.make_async_remote_copy(
                src_ref=held.at[slab, taken], dst_ref=held.at[slab, taken], send_sem=send.at[step], recv_sem=recv.at[step],
                device_id=(energy, partners[step - 1]), device_id_type=MESH,
            )
            for held, taken, send, recv in (
                (terms, pl.ds(0, POWERS), term_send, term_recv),
                (decays, pl.ds(0, 1), decay_send, decay_recv),
            )
        ]

    for step in range(1, slabs):

        @pl.when(partners[step - 1] > slab)
        def _():
            for copy in gathers(step):
                copy.start()

    kept = lines - EARLY
    shares = []
    for step in range(1, energies):
        copy = pltpu.make_async_remote_copy(
            src_ref=screened_ref.at[:, pl.ds(kept, EARLY), :], dst_ref=early.at[energy, :, pl.ds(kept, EARLY), :],
            send_sem=early_send.at[step], recv_sem=early_recv.at[step],
            device_id=(partner_of(energy, step, energies), slab), device_id_type=MESH,
        )
        copy.start()
        shares.append(copy)

    h4s = split(h4)
    lane = lax.broadcasted_iota(jnp.int32, (1, width), 1)
    inverses = [1.0 / (1.0 + k / total) for k in range(total)]
    load_rows.wait()

    def pick(places):
        chosen = [rows_ref[0, place] for place in places]
        v0 = jnp.concatenate([(lane == row).astype(jnp.float32) for row in chosen], axis=0)
        v1 = jnp.concatenate([hamilton[pl.ds(row, 1), :] for row in chosen], axis=0)
        v2 = jnp.concatenate([square[pl.ds(row, 1), :] for row in chosen], axis=0)
        v3 = mul(split(v1), h2s)
        lower = jnp.concatenate([v0, v1, v2, v3], axis=0)
        upper = mul(split(lower), h4s)
        v = [part[p * lines:(p + 1) * lines] for part in (lower, upper) for p in range(POWERS // 2)]
        picked = []
        for inverse in inverses:
            value = v[POWERS - 1]
            for p in reversed(range(POWERS - 1)):
                value = value * inverse + v[p]
            picked.append(value * inverse)
        return picked

    picked = pick([energy * lines + line for line in range(lines)])

    for step in range(1, slabs):

        @pl.when(partners[step - 1] < slab)
        def _():
            for copy in gathers(step):
                copy.wait_recv()

    carried = jnp.zeros((POWERS, width), jnp.float32)
    for place in range(slabs - 1):
        carried = jnp.where(place < slab, decays[place, 0:1] * carried + terms[place], carried)
    inverse_rows = 1.0 / (1.0 + lax.broadcasted_iota(jnp.int32, (total, width), 0).astype(jnp.float32) / total)
    incoming = jnp.broadcast_to(carried[POWERS - 1:], (total, width))
    for p in reversed(range(POWERS - 1)):
        incoming = incoming * inverse_rows + carried[p:p + 1]
    incoming = incoming * inverse_rows
    scale = 1.0 / (
        1.0 + (lax.broadcasted_iota(jnp.int32, (total * lines, width), 0) // lines).astype(jnp.float32) / total
    )
    scale2 = scale * scale

    def dress(picked):
        bare = jnp.concatenate(picked, axis=0)

        def store(value):
            value = value.reshape(total, lines, width)
            dressed[pl.ds(0, total)] = value
            dressed[pl.ds(total, total)] = value

        @pl.when(slab == 0)
        def _():
            store(bare)

        @pl.when(slab > 0)
        def _():
            u = jnp.concatenate([picked[k] * incoming[k:k + 1] for k in range(total)], axis=0)
            u = u + scale * mul(split(u), h1s)
            u = u + scale2 * mul(split(u), h2s)
            u = u + (scale2 * scale2) * mul(split(u), h4s)
            store(bare + scale * u)

    def convolve(place, held):
        first = place * share

        def add(m, acc):
            return acc + dressed[pl.ds(total + first - m, share)] * held[m][None]

        return lax.fori_loop(0, total, add, jnp.zeros((share, lines, width), jnp.float32), unroll=4)

    dress(picked)
    load_screen.wait()

    def pack(block):
        fill = jnp.concatenate(
            [jnp.zeros((kept, kept, width), jnp.float32)] + [block[k, :kept][:, None] for k in range(kept, share)], axis=1
        )
        line = lax.broadcasted_iota(jnp.int32, fill.shape, 1)
        return jnp.where(line < kept, block[:kept], fill)


    def deliver(slot, source, target):
        return pltpu.make_async_remote_copy(
            src_ref=sigma.at[slot], dst_ref=arrived.at[source],
            send_sem=sigma_send.at[slot], recv_sem=sigma_recv.at[source],
            device_id=(target, slab), device_id_type=MESH,
        )

    sends = []
    for slot in range(energies - 1):
        place = slot + (slot >= energy).astype(jnp.int32)
        sigma[slot] = pack(convolve(place, screen))
        copy = deliver(slot, energy, place)
        copy.start()
        sends.append(copy)
    arrived[energy] = pack(convolve(energy, screen))

    places = [place * lines + kept + line for place in range(energies) for line in range(EARLY)]
    dress(pick(places + [places[-1]] * (lines - len(places))))
    early[energy, :, pl.ds(kept, EARLY), :] = screen[:, kept:]
    for copy in shares:
        copy.wait()
    parts = [early[place, :, pl.ds(kept, EARLY), :] for place in range(energies)]
    parts += [jnp.zeros((total, lines - len(places), width), jnp.float32)] * (len(places) < lines)
    screen[...] = jnp.concatenate(parts, axis=1)
    result = convolve(energy, screen)
    for place in range(energies):
        out_ref[:, pl.ds(place * lines + kept, EARLY), :] = result[:, place * EARLY:(place + 1) * EARLY]

    for slot, copy in enumerate(sends):
        copy.wait_send()
        deliver(slot, slot + (slot >= energy).astype(jnp.int32), energy).wait_recv()
    for place in range(energies):
        first = place * lines
        out_ref[:kept, first:first + kept] = arrived[place, :, :kept]
        for k in range(kept, share):
            out_ref[k, first:first + kept] = arrived[place, :, k]
    for step in range(1, slabs):

        @pl.when(partners[step - 1] > slab)
        def _():
            for copy in gathers(step):
                copy.wait_send()


def fused(energies, slabs, hamiltonian, decay, coupling, rows, screened):
    total, lines, width = screened.shape
    share = total // energies
    dma = pltpu.SemaphoreType.DMA
    return pl.pallas_call(
        functools.partial(kernel, energies, slabs),
        out_shape=pltpu.VMEM((share, lines * energies, width), jnp.float32),
        in_specs=[pl.BlockSpec(memory_space=pltpu.HBM)] * 5,
        out_specs=pl.BlockSpec(memory_space=pltpu.VMEM),
        scratch_shapes=[
            pltpu.SMEM(rows.shape, jnp.int32),
            pltpu.VMEM(decay.shape, jnp.float32),
            pltpu.VMEM(coupling.shape, jnp.float32),
            pltpu.VMEM((width, width), jnp.float32),
            pltpu.VMEM((width, width), jnp.float32),
            pltpu.VMEM((total, lines, width), jnp.float32),
            pltpu.VMEM((energies, total, lines, width), jnp.float32),
            pltpu.VMEM((2 * total, lines, width), jnp.float32),
            pltpu.VMEM((energies, share - EARLY, lines, width), jnp.float32),
            pltpu.VMEM((energies, share - EARLY, lines, width), jnp.float32),
            pltpu.VMEM((slabs, POWERS, width), jnp.float32),
            pltpu.VMEM((slabs, POWERS, width), jnp.float32),
            dma((5,)),
            dma((slabs,)),
            dma((slabs,)),
            dma((slabs,)),
            dma((slabs,)),
            dma((energies,)),
            dma((energies,)),
            dma((energies,)),
            dma((energies,)),
        ],
        compiler_params=pltpu.CompilerParams(
            collective_id=0, has_side_effects=True, vmem_limit_bytes=60 * 1024 * 1024
        ),
    )(rows, decay, coupling, hamiltonian, screened)


def unfused(energies, slabs, hamiltonian, decay, coupling, rows, screened):
    total, lines, width = screened.shape
    share = total // energies
    dot = functools.partial(jnp.dot, precision=lax.Precision.HIGHEST)
    powers = [jnp.eye(width, dtype=jnp.float32)]
    for _ in range(POWERS - 1):
        powers.append(dot(powers[-1], hamiltonian))
    powers = jnp.stack(powers)
    own = coupling * jnp.diagonal(powers, axis1=1, axis2=2) / slabs
    decays = lax.all_gather(decay, "slab", axis=0, tiled=True)
    terms = lax.all_gather(own[None], "slab", axis=0, tiled=True)
    slab = lax.axis_index("slab")

    def advance(place, carried):
        return jnp.where(place < slab, decays[place] * carried + terms[place], carried)

    carried = lax.fori_loop(0, slabs - 1, advance, jnp.zeros_like(own))
    shifts = 1.0 + jnp.arange(total, dtype=jnp.int32).astype(jnp.float32) / total
    weights = shifts[:, None] ** -(1.0 + jnp.arange(POWERS, dtype=jnp.float32))
    incoming = dot(weights, carried)
    chosen = lax.dynamic_slice_in_dim(rows[0], lax.axis_index("energy") * lines, lines)
    picked = jnp.einsum("kp,prj->krj", weights, jnp.take(powers, chosen, axis=1), precision=lax.Precision.HIGHEST)
    scale = 1.0 / shifts[:, None, None]
    u = picked * incoming[:, None, :]
    u = u + scale * dot(u, powers[1])
    u = u + scale**2 * dot(u, powers[2])
    u = u + scale**4 * dot(u, powers[4])
    dressed = picked + scale * u

    def convolve(m, acc):
        return acc + jnp.roll(dressed, m, axis=0) * screened[m][None]

    sigma = lax.fori_loop(0, total, convolve, jnp.zeros_like(dressed))
    return lax.all_to_all(sigma, "energy", split_axis=0, concat_axis=1, tiled=True)


def solution(mesh):
    energies, slabs = mesh.shape["energy"], mesh.shape["slab"]

    def shards(hamiltonian, decay, coupling, rows, screened):
        lines = screened.shape[2]
        fits = lines == screened.shape[1] // energies == SUBLANES >= energies * EARLY and all(count & (count - 1) == 0 for count in (energies, slabs))
        form = fused if fits else unfused
        return form(energies, slabs, hamiltonian, decay, coupling, rows, screened[0])

    in_specs = (
        P("slab", None),
        P("slab", None),
        P("slab", None),
        P("slab", None),
        P("slab", None, "energy", None),
    )
    out_specs = P("energy", "slab", None)
    return jax.shard_map(shards, mesh=mesh, in_specs=in_specs, out_specs=out_specs, check_vma=False)
```

```python
import functools

import jax
import jax.numpy as jnp
from jax import lax
from jax.experimental import pallas as pl
from jax.experimental.pallas import tpu as pltpu
from jax.sharding import PartitionSpec as P

MESH = pl.DeviceIdType.MESH
POWERS = 8
SUBLANES = 8


def split(a):
    high = a.astype(jnp.bfloat16)
    return high, (a - high.astype(jnp.float32)).astype(jnp.bfloat16)


def mul(a, b):
    (a_high, a_low), (b_high, b_low) = a, b
    left = jnp.concatenate([a_low, a_high, a_high], axis=1)
    right = jnp.concatenate([b_high, b_low, b_high], axis=0)
    return jnp.dot(left, right, preferred_element_type=jnp.float32)


def partner_of(place, step, count):
    bit = 1
    while bit <= step:
        if step & bit:
            place = place + bit - 2 * bit * lax.rem(lax.div(place, bit), 2)
        bit *= 2
    return place


def kernel(
    energies, slabs, rows_hbm, decay_hbm, coupling_hbm, hamilton_ref, screened_ref, out_ref,
    rows_ref, decay_ref, coupling_ref, hamilton, square, screen, dressed, sigma, decays, terms,
    in_sem, decay_send, decay_recv, term_send, term_recv, sigma_send, sigma_recv,
):
    energy, slab = lax.axis_index("energy"), lax.axis_index("slab")
    total, lines, width = screen.shape
    share = total // energies

    loads = [
        pltpu.make_async_copy(source, held, in_sem.at[place])
        for place, (source, held) in enumerate(
            [
                (hamilton_ref, hamilton),
                (coupling_hbm, coupling_ref),
                (decay_hbm, decay_ref),
                (rows_hbm, rows_ref),
                (screened_ref, screen),
            ]
        )
    ]
    for load in loads:
        load.start()
    load_hamilton, load_coupling, load_decay, load_rows, load_screen = loads

    barrier = pltpu.get_barrier_semaphore()
    partners = [partner_of(slab, step, slabs) for step in range(1, slabs)]
    for partner in partners:

        @pl.when(partner < slab)
        def _():
            pl.semaphore_signal(barrier, inc=1, device_id=(energy, partner), device_id_type=MESH)

    for step in range(1, energies):
        pl.semaphore_signal(
            barrier, inc=1, device_id=(partner_of(energy, step, energies), slab), device_id_type=MESH
        )
    load_decay.wait()
    decays[slab] = jnp.broadcast_to(decay_ref[...], (POWERS, width))

    load_hamilton.wait()
    h1 = hamilton[...]
    t1 = h1.T
    h1s, t1s = split(h1), split(t1)
    h2 = mul(h1s, h1s)
    t2 = h2.T
    h2s, t2s = split(h2), split(t2)
    h4 = mul(h2s, h2s)
    t3 = mul(t2s, t1s)
    square[...] = h2

    def trace(product):
        return jnp.sum(product, axis=0, keepdims=True)

    eye = lax.broadcasted_iota(jnp.int32, h1.shape, 0) == lax.broadcasted_iota(jnp.int32, h1.shape, 1)
    diagonals = jnp.concatenate(
        [
            jnp.ones((1, width), jnp.float32),
            trace(jnp.where(eye, h1, 0.0)),
            trace(t1 * h1),
            trace(t1 * h2),
            trace(t2 * h2),
            trace(t1 * h4),
            trace(t2 * h4),
            trace(t3 * h4),
        ],
        axis=0,
    )
    load_coupling.wait()
    terms[slab] = diagonals * (coupling_ref[...] / slabs)

    pl.semaphore_wait(barrier, slabs - 1 - slab + energies - 1)

    def gathers(step):
        return [
            pltpu.make_async_remote_copy(
                src_ref=held.at[slab, taken], dst_ref=held.at[slab, taken], send_sem=send.at[step], recv_sem=recv.at[step],
                device_id=(energy, partners[step - 1]), device_id_type=MESH,
            )
            for held, taken, send, recv in (
                (terms, pl.ds(0, POWERS), term_send, term_recv),
                (decays, pl.ds(0, 1), decay_send, decay_recv),
            )
        ]

    for step in range(1, slabs):

        @pl.when(partners[step - 1] > slab)
        def _():
            for copy in gathers(step):
                copy.start()

    h4s = split(h4)
    lane = lax.broadcasted_iota(jnp.int32, (1, width), 1)
    inverses = [1.0 / (1.0 + k / total) for k in range(total)]
    load_rows.wait()

    def pick(places):
        chosen = [rows_ref[0, place] for place in places]
        v0 = jnp.concatenate([(lane == row).astype(jnp.float32) for row in chosen], axis=0)
        v1 = jnp.concatenate([hamilton[pl.ds(row, 1), :] for row in chosen], axis=0)
        v2 = jnp.concatenate([square[pl.ds(row, 1), :] for row in chosen], axis=0)
        v3 = mul(split(v1), h2s)
        lower = jnp.concatenate([v0, v1, v2, v3], axis=0)
        upper = mul(split(lower), h4s)
        v = [part[p * lines:(p + 1) * lines] for part in (lower, upper) for p in range(POWERS // 2)]
        picked = []
        for inverse in inverses:
            value = v[POWERS - 1]
            for p in reversed(range(POWERS - 1)):
                value = value * inverse + v[p]
            picked.append(value * inverse)
        return picked

    picked = pick([energy * lines + line for line in range(lines)])

    for step in range(1, slabs):

        @pl.when(partners[step - 1] < slab)
        def _():
            for copy in gathers(step):
                copy.wait_recv()

    carried = jnp.zeros((POWERS, width), jnp.float32)
    for place in range(slabs - 1):
        carried = jnp.where(place < slab, decays[place, 0:1] * carried + terms[place], carried)
    inverse_rows = 1.0 / (1.0 + lax.broadcasted_iota(jnp.int32, (total, width), 0).astype(jnp.float32) / total)
    incoming = jnp.broadcast_to(carried[POWERS - 1:], (total, width))
    for p in reversed(range(POWERS - 1)):
        incoming = incoming * inverse_rows + carried[p:p + 1]
    incoming = incoming * inverse_rows
    scale = 1.0 / (
        1.0 + (lax.broadcasted_iota(jnp.int32, (total * lines, width), 0) // lines).astype(jnp.float32) / total
    )
    scale2 = scale * scale

    def dress(picked):
        bare = jnp.concatenate(picked, axis=0)

        def store(value):
            value = value.reshape(total, lines, width)
            dressed[pl.ds(0, total)] = value
            dressed[pl.ds(total, total)] = value

        @pl.when(slab == 0)
        def _():
            store(bare)

        @pl.when(slab > 0)
        def _():
            u = jnp.concatenate([picked[k] * incoming[k:k + 1] for k in range(total)], axis=0)
            u = u + scale * mul(split(u), h1s)
            u = u + scale2 * mul(split(u), h2s)
            u = u + (scale2 * scale2) * mul(split(u), h4s)
            store(bare + scale * u)

    def convolve(place, held):
        first = place * share

        def add(m, acc):
            return acc + dressed[pl.ds(total + first - m, share)] * held[m][None]

        return lax.fori_loop(0, total, add, jnp.zeros((share, lines, width), jnp.float32), unroll=4)

    dress(picked)
    load_screen.wait()

    def lines_of(place):
        return pl.ds(pl.multiple_of(place * lines, SUBLANES), lines)

    def deliver(slot, source, target):
        return pltpu.make_async_remote_copy(
            src_ref=sigma.at[slot], dst_ref=out_ref.at[:, lines_of(source), :],
            send_sem=sigma_send.at[slot], recv_sem=sigma_recv.at[source],
            device_id=(target, slab), device_id_type=MESH,
        )

    sends = []
    for slot in range(energies - 1):
        place = slot + (slot >= energy).astype(jnp.int32)
        sigma[slot] = convolve(place, screen)
        copy = deliver(slot, energy, place)
        copy.start()
        sends.append(copy)
    out_ref[:, lines_of(energy), :] = convolve(energy, screen)

    for slot, copy in enumerate(sends):
        copy.wait_send()
        deliver(slot, slot + (slot >= energy).astype(jnp.int32), energy).wait_recv()
    for step in range(1, slabs):

        @pl.when(partners[step - 1] > slab)
        def _():
            for copy in gathers(step):
                copy.wait_send()


def fused(energies, slabs, hamiltonian, decay, coupling, rows, screened):
    total, lines, width = screened.shape
    share = total // energies
    dma = pltpu.SemaphoreType.DMA
    return pl.pallas_call(
        functools.partial(kernel, energies, slabs),
        out_shape=pltpu.VMEM((share, lines * energies, width), jnp.float32),
        in_specs=[pl.BlockSpec(memory_space=pltpu.HBM)] * 5,
        out_specs=pl.BlockSpec(memory_space=pltpu.VMEM),
        scratch_shapes=[
            pltpu.SMEM(rows.shape, jnp.int32),
            pltpu.VMEM(decay.shape, jnp.float32),
            pltpu.VMEM(coupling.shape, jnp.float32),
            pltpu.VMEM((width, width), jnp.float32),
            pltpu.VMEM((width, width), jnp.float32),
            pltpu.VMEM((total, lines, width), jnp.float32),
            pltpu.VMEM((2 * total, lines, width), jnp.float32),
            pltpu.VMEM((energies - 1, share, lines, width), jnp.float32),
            pltpu.VMEM((slabs, POWERS, width), jnp.float32),
            pltpu.VMEM((slabs, POWERS, width), jnp.float32),
            dma((5,)),
            dma((slabs,)),
            dma((slabs,)),
            dma((slabs,)),
            dma((slabs,)),
            dma((energies,)),
            dma((energies,)),
        ],
        compiler_params=pltpu.CompilerParams(
            collective_id=0, has_side_effects=True, vmem_limit_bytes=60 * 1024 * 1024
        ),
    )(rows, decay, coupling, hamiltonian, screened)


def unfused(energies, slabs, hamiltonian, decay, coupling, rows, screened):
    total, lines, width = screened.shape
    share = total // energies
    dot = functools.partial(jnp.dot, precision=lax.Precision.HIGHEST)
    powers = [jnp.eye(width, dtype=jnp.float32)]
    for _ in range(POWERS - 1):
        powers.append(dot(powers[-1], hamiltonian))
    powers = jnp.stack(powers)
    own = coupling * jnp.diagonal(powers, axis1=1, axis2=2) / slabs
    decays = lax.all_gather(decay, "slab", axis=0, tiled=True)
    terms = lax.all_gather(own[None], "slab", axis=0, tiled=True)
    slab = lax.axis_index("slab")

    def advance(place, carried):
        return jnp.where(place < slab, decays[place] * carried + terms[place], carried)

    carried = lax.fori_loop(0, slabs - 1, advance, jnp.zeros_like(own))
    shifts = 1.0 + jnp.arange(total, dtype=jnp.int32).astype(jnp.float32) / total
    weights = shifts[:, None] ** -(1.0 + jnp.arange(POWERS, dtype=jnp.float32))
    incoming = dot(weights, carried)
    chosen = lax.dynamic_slice_in_dim(rows[0], lax.axis_index("energy") * lines, lines)
    picked = jnp.einsum("kp,prj->krj", weights, jnp.take(powers, chosen, axis=1), precision=lax.Precision.HIGHEST)
    scale = 1.0 / shifts[:, None, None]
    u = picked * incoming[:, None, :]
    u = u + scale * dot(u, powers[1])
    u = u + scale**2 * dot(u, powers[2])
    u = u + scale**4 * dot(u, powers[4])
    dressed = picked + scale * u

    def convolve(m, acc):
        return acc + jnp.roll(dressed, m, axis=0) * screened[m][None]

    sigma = lax.fori_loop(0, total, convolve, jnp.zeros_like(dressed))
    return lax.all_to_all(sigma, "energy", split_axis=0, concat_axis=1, tiled=True)


def solution(mesh):
    energies, slabs = mesh.shape["energy"], mesh.shape["slab"]

    def shards(hamiltonian, decay, coupling, rows, screened):
        lines = screened.shape[2]
        fits = lines % SUBLANES == 0 and all(count & (count - 1) == 0 for count in (energies, slabs))
        form = fused if fits else unfused
        return form(energies, slabs, hamiltonian, decay, coupling, rows, screened[0])

    in_specs = (
        P("slab", None),
        P("slab", None),
        P("slab", None),
        P("slab", None),
        P("slab", None, "energy", None),
    )
    out_specs = P("energy", "slab", None)
    return jax.shard_map(shards, mesh=mesh, in_specs=in_specs, out_specs=out_specs, check_vma=False)
```

```python
import functools

import jax
import jax.numpy as jnp
from jax import lax
from jax.experimental import pallas as pl
from jax.experimental.pallas import tpu as pltpu
from jax.sharding import PartitionSpec as P

MESH = pl.DeviceIdType.MESH
POWERS = 8
SUBLANES = 8


def split(a):
    high = a.astype(jnp.bfloat16)
    return high, (a - high.astype(jnp.float32)).astype(jnp.bfloat16)


def mul(a, b):
    (a_high, a_low), (b_high, b_low) = a, b
    left = jnp.concatenate([a_low, a_high, a_high], axis=1)
    right = jnp.concatenate([b_high, b_low, b_high], axis=0)
    return jnp.dot(left, right, preferred_element_type=jnp.float32)


def partner_of(place, step, count):
    bit = 1
    while bit <= step:
        if step & bit:
            place = place + bit - 2 * bit * lax.rem(lax.div(place, bit), 2)
        bit *= 2
    return place


def kernel(
    energies, slabs, rows_hbm, decay_hbm, coupling_hbm, hamilton_ref, screened_ref, out_ref,
    rows_ref, decay_ref, coupling_ref, hamilton, square, screen, dressed, sigma, decays, terms,
    in_sem, decay_send, decay_recv, term_send, term_recv, sigma_send, sigma_recv,
):
    energy, slab = lax.axis_index("energy"), lax.axis_index("slab")
    total, lines, width = screen.shape
    share = total // energies

    loads = [
        pltpu.make_async_copy(source, held, in_sem.at[place])
        for place, (source, held) in enumerate(
            [
                (hamilton_ref, hamilton),
                (coupling_hbm, coupling_ref),
                (decay_hbm, decay_ref),
                (rows_hbm, rows_ref),
                (screened_ref, screen),
            ]
        )
    ]
    for load in loads:
        load.start()
    load_hamilton, load_coupling, load_decay, load_rows, load_screen = loads

    barrier = pltpu.get_barrier_semaphore()
    partners = [partner_of(slab, step, slabs) for step in range(1, slabs)]
    for partner in partners:

        @pl.when(partner < slab)
        def _():
            pl.semaphore_signal(barrier, inc=1, device_id=(energy, partner), device_id_type=MESH)

    for step in range(1, energies):
        pl.semaphore_signal(
            barrier, inc=1, device_id=(partner_of(energy, step, energies), slab), device_id_type=MESH
        )
    load_decay.wait()
    decays[slab] = jnp.broadcast_to(decay_ref[...], (POWERS, width))

    load_hamilton.wait()
    h1 = hamilton[...]
    t1 = h1.T
    h1s, t1s = split(h1), split(t1)
    h2 = mul(h1s, h1s)
    t2 = h2.T
    h2s, t2s = split(h2), split(t2)
    h4 = mul(h2s, h2s)
    t3 = mul(t2s, t1s)
    square[...] = h2

    def trace(product):
        return jnp.sum(product, axis=0, keepdims=True)

    eye = lax.broadcasted_iota(jnp.int32, h1.shape, 0) == lax.broadcasted_iota(jnp.int32, h1.shape, 1)
    diagonals = jnp.concatenate(
        [
            jnp.ones((1, width), jnp.float32),
            trace(jnp.where(eye, h1, 0.0)),
            trace(t1 * h1),
            trace(t1 * h2),
            trace(t2 * h2),
            trace(t1 * h4),
            trace(t2 * h4),
            trace(t3 * h4),
        ],
        axis=0,
    )
    load_coupling.wait()
    terms[slab] = diagonals * (coupling_ref[...] / slabs)

    pl.semaphore_wait(barrier, slabs - 1 - slab + energies - 1)

    def gathers(step):
        return [
            pltpu.make_async_remote_copy(
                src_ref=held.at[slab, taken], dst_ref=held.at[slab, taken], send_sem=send.at[step], recv_sem=recv.at[step],
                device_id=(energy, partners[step - 1]), device_id_type=MESH,
            )
            for held, taken, send, recv in (
                (terms, pl.ds(0, POWERS), term_send, term_recv),
                (decays, pl.ds(0, 1), decay_send, decay_recv),
            )
        ]

    for kind in range(2):
        for step in range(1, slabs):

            @pl.when(partners[step - 1] > slab)
            def _():
                gathers(step)[kind].start()

    h4s = split(h4)
    lane = lax.broadcasted_iota(jnp.int32, (1, width), 1)
    inverses = [1.0 / (1.0 + k / total) for k in range(total)]
    load_rows.wait()

    def pick(places):
        chosen = [rows_ref[0, place] for place in places]
        v0 = jnp.concatenate([(lane == row).astype(jnp.float32) for row in chosen], axis=0)
        v1 = jnp.concatenate([hamilton[pl.ds(row, 1), :] for row in chosen], axis=0)
        v2 = jnp.concatenate([square[pl.ds(row, 1), :] for row in chosen], axis=0)
        v3 = mul(split(v1), h2s)
        lower = jnp.concatenate([v0, v1, v2, v3], axis=0)
        upper = mul(split(lower), h4s)
        v = [part[p * lines:(p + 1) * lines] for part in (lower, upper) for p in range(POWERS // 2)]
        picked = []
        for inverse in inverses:
            value = v[POWERS - 1]
            for p in reversed(range(POWERS - 1)):
                value = value * inverse + v[p]
            picked.append(value * inverse)
        return picked

    picked = pick([energy * lines + line for line in range(lines)])

    for step in range(1, slabs):

        @pl.when(partners[step - 1] < slab)
        def _():
            for copy in gathers(step):
                copy.wait_recv()

    carried = jnp.zeros((POWERS, width), jnp.float32)
    for place in range(slabs - 1):
        carried = jnp.where(place < slab, decays[place, 0:1] * carried + terms[place], carried)
    inverse_rows = 1.0 / (1.0 + lax.broadcasted_iota(jnp.int32, (total, width), 0).astype(jnp.float32) / total)
    incoming = jnp.broadcast_to(carried[POWERS - 1:], (total, width))
    for p in reversed(range(POWERS - 1)):
        incoming = incoming * inverse_rows + carried[p:p + 1]
    incoming = incoming * inverse_rows
    scale = 1.0 / (
        1.0 + (lax.broadcasted_iota(jnp.int32, (total * lines, width), 0) // lines).astype(jnp.float32) / total
    )
    scale2 = scale * scale

    def dress(picked):
        bare = jnp.concatenate(picked, axis=0)

        def store(value):
            value = value.reshape(total, lines, width)
            dressed[pl.ds(0, total)] = value
            dressed[pl.ds(total, total)] = value

        @pl.when(slab == 0)
        def _():
            store(bare)

        @pl.when(slab > 0)
        def _():
            u = jnp.concatenate([picked[k] * incoming[k:k + 1] for k in range(total)], axis=0)
            u = u + scale * mul(split(u), h1s)
            u = u + scale2 * mul(split(u), h2s)
            u = u + (scale2 * scale2) * mul(split(u), h4s)
            store(bare + scale * u)

    def convolve(place, held):
        first = place * share

        def add(m, acc):
            return acc + dressed[pl.ds(total + first - m, share)] * held[m][None]

        return lax.fori_loop(0, total, add, jnp.zeros((share, lines, width), jnp.float32), unroll=4)

    dress(picked)
    load_screen.wait()

    def lines_of(place):
        return pl.ds(pl.multiple_of(place * lines, SUBLANES), lines)

    def deliver(slot, source, target):
        return pltpu.make_async_remote_copy(
            src_ref=sigma.at[slot], dst_ref=out_ref.at[:, lines_of(source), :],
            send_sem=sigma_send.at[slot], recv_sem=sigma_recv.at[source],
            device_id=(target, slab), device_id_type=MESH,
        )

    sends = []
    for slot in range(energies - 1):
        place = slot + (slot >= energy).astype(jnp.int32)
        sigma[slot] = convolve(place, screen)
        copy = deliver(slot, energy, place)
        copy.start()
        sends.append(copy)
    out_ref[:, lines_of(energy), :] = convolve(energy, screen)

    for slot, copy in enumerate(sends):
        copy.wait_send()
        deliver(slot, slot + (slot >= energy).astype(jnp.int32), energy).wait_recv()
    for step in range(1, slabs):

        @pl.when(partners[step - 1] > slab)
        def _():
            for copy in gathers(step):
                copy.wait_send()


def fused(energies, slabs, hamiltonian, decay, coupling, rows, screened):
    total, lines, width = screened.shape
    share = total // energies
    dma = pltpu.SemaphoreType.DMA
    return pl.pallas_call(
        functools.partial(kernel, energies, slabs),
        out_shape=pltpu.VMEM((share, lines * energies, width), jnp.float32),
        in_specs=[pl.BlockSpec(memory_space=pltpu.HBM)] * 5,
        out_specs=pl.BlockSpec(memory_space=pltpu.VMEM),
        scratch_shapes=[
            pltpu.SMEM(rows.shape, jnp.int32),
            pltpu.VMEM(decay.shape, jnp.float32),
            pltpu.VMEM(coupling.shape, jnp.float32),
            pltpu.VMEM((width, width), jnp.float32),
            pltpu.VMEM((width, width), jnp.float32),
            pltpu.VMEM((total, lines, width), jnp.float32),
            pltpu.VMEM((2 * total, lines, width), jnp.float32),
            pltpu.VMEM((energies - 1, share, lines, width), jnp.float32),
            pltpu.VMEM((slabs, POWERS, width), jnp.float32),
            pltpu.VMEM((slabs, POWERS, width), jnp.float32),
            dma((5,)),
            dma((slabs,)),
            dma((slabs,)),
            dma((slabs,)),
            dma((slabs,)),
            dma((energies,)),
            dma((energies,)),
        ],
        compiler_params=pltpu.CompilerParams(
            collective_id=0, has_side_effects=True, vmem_limit_bytes=60 * 1024 * 1024
        ),
    )(rows, decay, coupling, hamiltonian, screened)


def unfused(energies, slabs, hamiltonian, decay, coupling, rows, screened):
    total, lines, width = screened.shape
    share = total // energies
    dot = functools.partial(jnp.dot, precision=lax.Precision.HIGHEST)
    powers = [jnp.eye(width, dtype=jnp.float32)]
    for _ in range(POWERS - 1):
        powers.append(dot(powers[-1], hamiltonian))
    powers = jnp.stack(powers)
    own = coupling * jnp.diagonal(powers, axis1=1, axis2=2) / slabs
    decays = lax.all_gather(decay, "slab", axis=0, tiled=True)
    terms = lax.all_gather(own[None], "slab", axis=0, tiled=True)
    slab = lax.axis_index("slab")

    def advance(place, carried):
        return jnp.where(place < slab, decays[place] * carried + terms[place], carried)

    carried = lax.fori_loop(0, slabs - 1, advance, jnp.zeros_like(own))
    shifts = 1.0 + jnp.arange(total, dtype=jnp.int32).astype(jnp.float32) / total
    weights = shifts[:, None] ** -(1.0 + jnp.arange(POWERS, dtype=jnp.float32))
    incoming = dot(weights, carried)
    chosen = lax.dynamic_slice_in_dim(rows[0], lax.axis_index("energy") * lines, lines)
    picked = jnp.einsum("kp,prj->krj", weights, jnp.take(powers, chosen, axis=1), precision=lax.Precision.HIGHEST)
    scale = 1.0 / shifts[:, None, None]
    u = picked * incoming[:, None, :]
    u = u + scale * dot(u, powers[1])
    u = u + scale**2 * dot(u, powers[2])
    u = u + scale**4 * dot(u, powers[4])
    dressed = picked + scale * u

    def convolve(m, acc):
        return acc + jnp.roll(dressed, m, axis=0) * screened[m][None]

    sigma = lax.fori_loop(0, total, convolve, jnp.zeros_like(dressed))
    return lax.all_to_all(sigma, "energy", split_axis=0, concat_axis=1, tiled=True)


def solution(mesh):
    energies, slabs = mesh.shape["energy"], mesh.shape["slab"]

    def shards(hamiltonian, decay, coupling, rows, screened):
        lines = screened.shape[2]
        fits = lines % SUBLANES == 0 and all(count & (count - 1) == 0 for count in (energies, slabs))
        form = fused if fits else unfused
        return form(energies, slabs, hamiltonian, decay, coupling, rows, screened[0])

    in_specs = (
        P("slab", None),
        P("slab", None),
        P("slab", None),
        P("slab", None),
        P("slab", None, "energy", None),
    )
    out_specs = P("energy", "slab", None)
    return jax.shard_map(shards, mesh=mesh, in_specs=in_specs, out_specs=out_specs, check_vma=False)
```
